256 devices in a mesh: atom: 64 (over z, y_hi, x), wave: 4 (over y_lo, core).
Axes of the slice: x: 4, y: 4 (y_hi: 2, y_lo: 2; y = y_hi * 2 + y_lo), z: 8, core: 2. Of those that a mesh axis runs over, the one named last changes fastest.
Arguments:
- positions: float32 [3, 262144], P(None, 'atom'), may hold values from 0 to 256
- features: bfloat16 [262144, 128], P('atom'), may hold values from -6 to 6
- cotangent: bfloat16 [262144, 128], P('atom'), may hold values from -6 to 6
- miller: int32 [3, 4096], P(None, 'wave'), may hold values from -8 to 8
- radial_filter: float32 [4096, 128], P('wave'), may hold values from 0.3 to 3
Outputs:
- feature_grad: float32 [262144, 128], P('atom')
- position_grad: float32 [3, 262144], P(None, 'atom')
- filter_grad: float32 [4096, 128], P('wave')
The draws below stay inside these ranges and needn't reach their ends.
All inputs are finite; a program needn't handle non-finite values.
Results may differ from the reference program's by a relative error of at most 0.008.
Values sent between devices are 32-bit elements; how exact they have to be, the bound alone decides.
No kernel may reach another device: no remote copies, remote signals or barrier semaphores. Data moves between devices by JAX's collectives and lax.ppermute only.
A program may use at most 128 MiB of HBM per device.

```python
import math
import jax
import jax.numpy as jnp
from jax import lax

C = 128
K = 4096
ATOMS = 262144


def with_ends(result, stream_key, low, largest):
    spot = [jax.random.randint(jax.random.fold_in(stream_key, axis), (), 0, length) for axis, length in enumerate(result.shape)]
    main_axis = result.shape.index(max(result.shape))
    neighbour = spot[:main_axis] + [(spot[main_axis] + 1) % result.shape[main_axis]] + spot[main_axis + 1:]
    return result.at[tuple(spot)].set(low).at[tuple(neighbour)].set(largest)


def block_scale(key, shape, split, least, largest):
    def one(axis_at, blocks):
        heights = jax.random.uniform(jax.random.fold_in(jax.random.fold_in(key, 6), axis_at), (blocks,), jnp.float32, least / len(split), largest / len(split))
        return jnp.repeat(jnp.exp(heights), shape[axis_at] // blocks).reshape((-1,) + (1,) * (len(shape) - axis_at - 1))

    level = one(*split[0])
    for cut in split[1:]:
        level = level * one(*cut)
    return level


def gaussian(stream_key, shape, width, reach, cuts=(), dtype=jnp.bfloat16):
    factor_of = block_scale(stream_key, shape, cuts, -0.22, 0.18) if cuts else 1.0
    entries = jax.random.normal(stream_key, shape, jnp.float32) * width * factor_of
    return jnp.minimum(jnp.maximum(entries, -reach), reach).astype(dtype)


def setup_inputs(seed: int = 0) -> dict:
    key_list = jax.random.split(jax.random.key(seed), 6)
    return {
        "positions": jnp.clip(256.0 * jax.random.uniform(key_list[0], (3, ATOMS), jnp.float32) ** block_scale(key_list[0], (3, ATOMS), ((1, 64),), -0.2, 0.2), 0.0, 256.0),
        "features": gaussian(key_list[1], (ATOMS, C), 1.0, 6.0, ((0, 64),)),
        "cotangent": gaussian(key_list[2], (ATOMS, C), 1.0, 6.0, ((0, 64),)),
        "miller": with_ends(jax.random.randint(key_list[3], (3, K), -8, 9), jax.random.fold_in(key_list[3], 1), -8, 8).astype(jnp.int32),
        "radial_filter": jnp.clip(jnp.exp(math.log(3.0) - 2.3025851 * jax.random.uniform(key_list[4], (K, C), jnp.float32) ** block_scale(key_list[4], (K, C), ((0, 4),), -0.2, 0.2)), 0.3, 3.0),
    }


phase_step = 2.0 * math.pi / 256.0


def trig_pair(place, indices):
    millers = indices.astype(jnp.float32)
    theta = phase_step * (place[0][:, None] * millers[0][None, :] + place[1][:, None] * millers[1][None, :] + place[2][:, None] * millers[2][None, :])
    return jnp.cos(theta).astype(jnp.bfloat16), jnp.sin(theta).astype(jnp.bfloat16)


def reference(positions, features, cotangent, miller, radial_filter):
    block = math.gcd(ATOMS, 4096)
    blocks = ATOMS // block
    pos_blocks = positions.reshape(3, blocks, block).transpose(1, 0, 2)
    joined_rows = jnp.concatenate([features, cotangent], 1).reshape(blocks, block, 2 * C)

    def accumulate(total, item):
        place, rows = item
        cosine, sine = trig_pair(place, miller)
        tables = jnp.concatenate([cosine, sine], 1)
        return total + lax.dot_general(tables, rows, (((0,), (0,)), ((), ())), preferred_element_type=jnp.float32), None

    product, _ = lax.scan(accumulate, jnp.zeros((2 * K, 2 * C), jnp.float32), (pos_blocks, joined_rows))
    factor_sc = product[:K, :C]
    factor_gc = product[:K, C:]
    factor_ss = product[K:, :C]
    factor_gs = product[K:, C:]
    scale = float(ATOMS * K) ** -0.5
    filter_grad = scale * (factor_gc * factor_sc + factor_gs * factor_ss)
    weighted = radial_filter * scale
    w_sc = (weighted * factor_sc).astype(jnp.bfloat16)
    w_gc = (weighted * factor_gc).astype(jnp.bfloat16)
    w_ss = (weighted * factor_ss).astype(jnp.bfloat16)
    w_gs = (weighted * factor_gs).astype(jnp.bfloat16)
    down_table = jnp.concatenate([w_gc, w_gs], 0)
    right_table = jnp.concatenate([jnp.concatenate([w_gs, w_gc], 0), jnp.concatenate([w_ss, w_sc], 0)], 1)
    miller_rows = miller.astype(jnp.bfloat16)

    def gradients(item):
        place, rows = item
        cosine, sine = trig_pair(place, miller)
        tables = jnp.concatenate([cosine, sine], 1)
        feat_part = jnp.dot(tables, down_table, preferred_element_type=jnp.float32)
        pq_table = lax.dot_general(rows, right_table, (((1,), (1,)), ((), ())), preferred_element_type=jnp.float32)
        dtheta = (cosine.astype(jnp.float32) * pq_table[:, :K] - sine.astype(jnp.float32) * pq_table[:, K:]).astype(jnp.bfloat16)
        pos_part = phase_step * lax.dot_general(miller_rows, dtheta, (((1,), (1,)), ((), ())), preferred_element_type=jnp.float32)
        return feat_part, pos_part

    feat_blocks, pos_parts = lax.map(gradients, (pos_blocks, joined_rows))
    feature_grad = feat_blocks.reshape(ATOMS, C)
    position_grad = pos_parts.transpose(1, 0, 2).reshape(3, ATOMS)
    return feature_grad, position_grad, filter_grad
```

```python
import functools
import math

import jax
import jax.numpy as jnp
from jax import lax
from jax.experimental import pallas as pl
from jax.experimental.pallas import tpu as pltpu
from jax.sharding import Mesh, PartitionSpec as P

phase_step = 2.0 * math.pi / 256.0
PAIRS = 296
PAIR_ROWS = 304
TILES = 9
SLOTS = 17 * 64
CLASSES = 896
PACKED = 2560
f32 = jnp.float32
bf16 = jnp.bfloat16
VMEM_LIMIT = 56 * 1024 * 1024


def nt_dot(a, b):
    return lax.dot_general(a, b, (((1,), (1,)), ((), ())), preferred_element_type=f32)


def turn_trig(turns):
    x = (turns - jnp.floor(turns + 0.5)) * (2.0 * math.pi)
    square = x * x
    cosine = jnp.full_like(x, 1.0 / math.factorial(18) * -1.0)
    for power in range(16, -1, -2):
        cosine = cosine * square + ((-1.0) ** (power // 2) / math.factorial(power))
    sine = jnp.full_like(x, 1.0 / math.factorial(17))
    for power in range(15, 0, -2):
        sine = sine * square + ((-1.0) ** (power // 2) / math.factorial(power))
    return cosine, sine * x


def multiples(position_rows):
    count = position_rows.shape[1]
    orders = lax.broadcasted_iota(jnp.int32, (8, count), 0).astype(f32) + 1.0
    return [turn_trig(orders * (position_rows[d : d + 1, :] * (1.0 / 256.0))) for d in range(3)]


def pair_table(trig1, trig2):
    (c1, s1), (c2, s2) = trig1, trig2
    count = c1.shape[1]
    tiles = []
    for left in (c1, s1):
        for right in (c2, s2):
            for m in range(8):
                tiles.append(left[m : m + 1, :] * right)
    one = (lax.broadcasted_iota(jnp.int32, (16, count), 0) == 0).astype(f32)
    tiles += [c2, s2, c1, s1, one]
    return jnp.concatenate(tiles, 0)


def row_tables(pick_ref, features, cotangent):
    lane = lax.broadcasted_iota(jnp.int32, (32, 128), 1)
    row = lax.broadcasted_iota(jnp.int32, (32, 128), 0)
    pick = (lane == row + 32 * pick_ref[0]).astype(bf16)
    return jnp.concatenate([nt_dot(pick, features), nt_dot(pick, cotangent)], 0)


def fill_slots(slots_ref, trig0, rows):
    c0, s0 = trig0
    for t in range(8):
        slots_ref[128 * t : 128 * t + 64, :] = (c0[t : t + 1, :] * rows).astype(bf16)
        slots_ref[128 * t + 64 : 128 * t + 128, :] = (s0[t : t + 1, :] * rows).astype(bf16)
    slots_ref[1024:1088, :] = rows.astype(bf16)


def factor_kernel(pick_ref, pos_ref, feat_ref, cot_ref, out_ref, slots_ref, total_ref):
    step = pl.program_id(0)
    trig = multiples(pos_ref[...])
    fill_slots(slots_ref, trig[0], row_tables(pick_ref, feat_ref[...], cot_ref[...]))
    pairs = pair_table(trig[1], trig[2]).astype(bf16)
    product = nt_dot(pairs, slots_ref[...])

    @pl.when(step == 0)
    def _():
        total_ref[...] = product

    @pl.when(step > 0)
    def _():
        total_ref[...] += product

    @pl.when(step == pl.num_programs(0) - 1)
    def _():
        for t in range(8):
            out_ref[PAIRS * t : PAIRS * (t + 1), :] = total_ref[0:PAIRS, 128 * t : 128 * t + 128]
        last = total_ref[:, 1024:1088]
        out_ref[2368:2520, :] = jnp.concatenate([last[0:152], last[152:304]], 1)
        out_ref[2520:2560, :] = jnp.zeros((40, 128), f32)


def factors(pick, positions, features, cotangent, block):
    atoms = positions.shape[1]
    return pl.pallas_call(
        factor_kernel,
        grid=(atoms // block,),
        in_specs=[
            pl.BlockSpec(memory_space=pltpu.SMEM),
            pl.BlockSpec((3, block), lambda i: (0, i)),
            pl.BlockSpec((block, 128), lambda i: (i, 0)),
            pl.BlockSpec((block, 128), lambda i: (i, 0)),
        ],
        out_specs=pl.BlockSpec((PACKED, 128), lambda i: (0, 0)),
        out_shape=jax.ShapeDtypeStruct((PACKED, 128), f32),
        scratch_shapes=[pltpu.VMEM((SLOTS, block), bf16), pltpu.VMEM((PAIR_ROWS, SLOTS), f32)],
        compiler_params=pltpu.CompilerParams(vmem_limit_bytes=VMEM_LIMIT),
        cost_estimate=pl.CostEstimate(flops=2 * PAIR_ROWS * SLOTS * atoms, bytes_accessed=atoms * 520, transcendentals=0),
        name="factors",
    )(pick, positions, features, cotangent)


def wave_class(m):
    m0, m1, m2 = [m[d : d + 1, :] for d in range(3)]
    size0, size1, size2 = jnp.abs(m0), jnp.abs(m1), jnp.abs(m2)
    signs = [jnp.clip(v, -1.0, 1.0) for v in (m0, m1, m2)]
    both = (size1 - 1.0) * 8.0 + size2 - 1.0
    inner = jnp.where(
        size1 > 0.0,
        jnp.where(size2 > 0.0, both, 72.0 + size1 - 1.0),
        jnp.where(size2 > 0.0, 64.0 + size2 - 1.0, 80.0),
    )
    tile = jnp.where(size0 > 0.0, size0 - 1.0, 8.0)
    index = (tile * 88.0 + inner).astype(jnp.int32)
    return index, (signs[1] * signs[2], signs[0] * signs[1], signs[0] * signs[2])


def split_hi_lo(v):
    hi = v.astype(bf16)
    return hi, (v - hi.astype(f32)).astype(bf16)


def class_kernel(miller_ref, radial_ref, out_ref):
    step = pl.program_id(0)
    index, products = wave_class(miller_ref[0:3, :])
    radial = radial_ref[...]
    signed = jnp.concatenate([radial] + [radial * p for p in products], 0)
    hi, lo = split_hi_lo(signed)
    hot = (lax.broadcasted_iota(jnp.int32, (CLASSES, index.shape[1]), 0) == index).astype(f32).astype(bf16)
    part = nt_dot(hot, jnp.concatenate([hi, lo], 0))
    part = part[:, :128] + part[:, 128:]

    @pl.when(step == 0)
    def _():
        out_ref[...] = part

    @pl.when(step > 0)
    def _():
        out_ref[...] += part


def class_sums(miller_rows, radial_rows, block):
    waves = miller_rows.shape[1]
    return pl.pallas_call(
        class_kernel,
        grid=(waves // block,),
        in_specs=[pl.BlockSpec((8, block), lambda i: (0, i)), pl.BlockSpec((32, block), lambda i: (0, i))],
        out_specs=pl.BlockSpec((CLASSES, 128), lambda i: (0, 0)),
        out_shape=jax.ShapeDtypeStruct((CLASSES, 128), f32),
        compiler_params=pltpu.CompilerParams(vmem_limit_bytes=VMEM_LIMIT),
        cost_estimate=pl.CostEstimate(flops=2 * CLASSES * 256 * waves, bytes_accessed=waves * 160, transcendentals=0),
        name="class_sums",
    )(miller_rows, radial_rows)


def spread(x, q):
    part = x[:, 32 * q : 32 * q + 32]
    return jnp.concatenate([part, part, part, part], 1)


def combine_kernel(scale, total_ref, class_ref, uv_ref, down_ref, pair_ref):
    lane = lax.broadcasted_iota(jnp.int32, (1, 128), 1)
    half = jnp.where(lane < 64, 1.0, -1.0).astype(f32)
    swap = (lane % 64) < 32
    pick_lane = lax.broadcasted_iota(jnp.int32, (64, 128), 1)
    pick_row = lax.broadcasted_iota(jnp.int32, (64, 128), 0)
    pick = (pick_lane == jnp.where(pick_row < 32, pick_row + 32, pick_row + 64)).astype(bf16)
    pair_ref[...] = jnp.zeros((CLASSES, 128), f32)
    for t in range(TILES):
        if t < 8:
            a = total_ref[PAIRS * t : PAIRS * (t + 1), :]
        else:
            fold = total_ref[2368:2520, :]
            a = jnp.concatenate([fold[:, :64], fold[0:144, 64:]], 0)
            a = jnp.concatenate([a, jnp.zeros((PAIRS, 64), f32)], 1)
        b = half * pltpu.roll(a, 64, 1)
        sa = pltpu.roll(a, 32, 1)
        sb = pltpu.roll(b, 32, 1)
        x = class_ref[88 * t : 88 * t + 88, :] * scale
        x0, x1, x2, x3 = [spread(x, q) for q in range(4)]
        i0, i1, i2, i3 = [v[0:64] for v in (x0, x1, x2, x3)]
        cut = lambda v: [v[0:64], v[64:128], v[128:192], v[192:256]] + [v[256 + 8 * k : 264 + 8 * k] for k in range(5)]
        cc, cs, sc, ss, e2c, e2s, e1c, e1s, co = cut(a)
        bcc, bcs, bsc, bss, be2c, be2s, be1c, be1s, _ = cut(b)
        f0, f3 = x0[64:72], x3[64:72]
        g0, g2 = x0[72:80], x2[72:80]
        w = jnp.concatenate(
            [
                i0 * cc - i1 * ss - i2 * bsc - i3 * bcs,
                i0 * cs + i1 * sc - i2 * bss + i3 * bcc,
                i0 * sc + i1 * cs + i2 * bcc - i3 * bss,
                i0 * ss - i1 * cc + i2 * bcs + i3 * bsc,
                f0 * e2c - f3 * be2s,
                f0 * e2s + f3 * be2c,
                g0 * e1c - g2 * be1s,
                g0 * e1s + g2 * be1c,
                x0[80:88] * co,
                jnp.zeros((8, 128), f32),
            ],
            0,
        )
        swapped = jnp.where(swap, pltpu.roll(w, 96, 1), pltpu.roll(w, 32, 1))
        uv_ref[0:PAIR_ROWS, 128 * t : 128 * t + 128] = swapped.astype(bf16)
        slope = float(t + 1 if t < 8 else 0)
        uv_ref[PAIR_ROWS : 2 * PAIR_ROWS, 128 * t : 128 * t + 128] = (
            (slope * half) * pltpu.roll(swapped, 64, 1)
        ).astype(bf16)
        down_ref[64 * t : 64 * t + 64, :] = nt_dot(pick, w.astype(bf16)).astype(bf16)
        scc, scs, ssc, sss, se2c, se2s, se1c, se1s, sco = cut(sa)
        tcc, tcs, tsc, tss, te2c, te2s, te1c, te1s, _ = cut(sb)
        zero = jnp.zeros((8, 128), f32)
        y = [
            [cc * scc + cs * scs + sc * ssc + ss * sss, e2c * se2c + e2s * se2s, e1c * se1c + e1s * se1s, co * sco],
            [cs * ssc + sc * scs - cc * sss - ss * scc, zero, zero, zero],
            [sc * tcc + ss * tcs - cc * tsc - cs * tss, zero, e1s * te1c - e1c * te1s, zero],
            [cs * tcc + ss * tsc - cc * tcs - sc * tss, e2s * te2c - e2c * te2s, zero, zero],
        ]
        parts = []
        for q in range(4):
            z = jnp.concatenate(y[q], 0)
            parts.append(z[:, 32:64] + z[:, 96:128])
        pair_ref[88 * t : 88 * t + 88, :] = jnp.concatenate(parts, 1)


def combine(total, classes, scale):
    return pl.pallas_call(
        functools.partial(combine_kernel, scale),
        out_shape=(
            jax.ShapeDtypeStruct((2 * PAIR_ROWS, 128 * TILES), bf16),
            jax.ShapeDtypeStruct((64 * TILES, PAIR_ROWS), bf16),
            jax.ShapeDtypeStruct((CLASSES, 128), f32),
        ),
        compiler_params=pltpu.CompilerParams(vmem_limit_bytes=VMEM_LIMIT),
        name="combine",
    )(total, classes)


def filter_kernel(scale, miller_ref, pair_ref, out_ref):
    index, products = wave_class(miller_ref[0:3, :])
    hot = (lax.broadcasted_iota(jnp.int32, (CLASSES, index.shape[1]), 0) == index).astype(f32).astype(bf16)
    turned = pair_ref[...].T
    hi, lo = split_hi_lo(turned)
    values = jnp.dot(jnp.concatenate([hi, lo], 0), hot, preferred_element_type=f32)
    values = values[:128] + values[128:]
    total = values[0:32]
    for q in range(3):
        total = total + products[q] * values[32 * (q + 1) : 32 * (q + 2)]
    out_ref[...] = scale * total


def filter_rows(miller_rows, pair_products, scale, block):
    waves = miller_rows.shape[1]
    return pl.pallas_call(
        functools.partial(filter_kernel, scale),
        grid=(waves // block,),
        in_specs=[pl.BlockSpec((8, block), lambda i: (0, i)), pl.BlockSpec((CLASSES, 128), lambda i: (0, 0))],
        out_specs=pl.BlockSpec((32, block), lambda i: (0, i)),
        out_shape=jax.ShapeDtypeStruct((32, waves), f32),
        compiler_params=pltpu.CompilerParams(vmem_limit_bytes=VMEM_LIMIT),
        cost_estimate=pl.CostEstimate(flops=2 * CLASSES * 256 * waves, bytes_accessed=waves * 160, transcendentals=0),
        name="filter_rows",
    )(miller_rows, pair_products)


def gradient_kernel(pick_ref, pos_ref, feat_ref, cot_ref, uv_ref, down_ref, grad_ref, posg_ref, slots_ref):
    trig = multiples(pos_ref[...])
    (c0, s0), (c1, s1), (c2, s2) = trig
    fill_slots(slots_ref, trig[0], row_tables(pick_ref, feat_ref[...], cot_ref[...]))
    pairs = pair_table(trig[1], trig[2]).astype(bf16)
    parts = jnp.dot(down_ref[...], pairs, preferred_element_type=f32)
    grad = parts[512:544]
    for t in range(8):
        grad = grad + c0[t : t + 1, :] * parts[64 * t : 64 * t + 32] + s0[t : t + 1, :] * parts[64 * t + 32 : 64 * t + 64]
    grad_ref[...] = grad
    both = jnp.dot(uv_ref[:, 0:SLOTS], slots_ref[...], preferred_element_type=f32)
    u = both[0:PAIR_ROWS]
    v = both[PAIR_ROWS:]
    orders = lax.broadcasted_iota(jnp.int32, c1.shape, 0).astype(f32) + 1.0
    acc0 = c2 * v[256:264] + s2 * v[264:272] + c1 * v[272:280] + s1 * v[280:288]
    acc1 = orders * (c1 * u[280:288] - s1 * u[272:280])
    acc2 = c2 * u[264:272] - s2 * u[256:264]
    for m in range(8):
        lead_c, lead_s = c1[m : m + 1, :], s1[m : m + 1, :]
        ucc, ucs, usc, uss = [u[64 * k + 8 * m : 64 * k + 8 * m + 8] for k in range(4)]
        vcc, vcs, vsc, vss = [v[64 * k + 8 * m : 64 * k + 8 * m + 8] for k in range(4)]
        acc0 = acc0 + lead_c * (c2 * vcc + s2 * vcs) + lead_s * (c2 * vsc + s2 * vss)
        acc1 = acc1 + float(m + 1) * (lead_c * (c2 * usc + s2 * uss) - lead_s * (c2 * ucc + s2 * ucs))
        acc2 = acc2 + lead_c * (c2 * ucs - s2 * ucc) + lead_s * (c2 * uss - s2 * usc)
    acc2 = acc2 * orders
    rows = [jnp.sum(acc0, 0, keepdims=True) + v[288:289], jnp.sum(acc1, 0, keepdims=True), jnp.sum(acc2, 0, keepdims=True)]
    posg_ref[...] = phase_step * jnp.concatenate(rows, 0)


def gradients(pick, positions, features, cotangent, uv, down, block):
    atoms = positions.shape[1]
    return pl.pallas_call(
        gradient_kernel,
        grid=(atoms // block,),
        in_specs=[
            pl.BlockSpec(memory_space=pltpu.SMEM),
            pl.BlockSpec((3, block), lambda i: (0, i)),
            pl.BlockSpec((block, 128), lambda i: (i, 0)),
            pl.BlockSpec((block, 128), lambda i: (i, 0)),
            pl.BlockSpec((2 * PAIR_ROWS, 128 * TILES), lambda i: (0, 0)),
            pl.BlockSpec((64 * TILES, PAIR_ROWS), lambda i: (0, 0)),
        ],
        out_specs=(pl.BlockSpec((32, block), lambda i: (0, i)), pl.BlockSpec((3, block), lambda i: (0, i))),
        out_shape=(jax.ShapeDtypeStruct((32, atoms), f32), jax.ShapeDtypeStruct((3, atoms), f32)),
        scratch_shapes=[pltpu.VMEM((SLOTS, block), bf16)],
        compiler_params=pltpu.CompilerParams(vmem_limit_bytes=VMEM_LIMIT),
        cost_estimate=pl.CostEstimate(flops=6 * PAIR_ROWS * SLOTS * atoms, bytes_accessed=atoms * 700, transcendentals=0),
        name="gradients",
    )(pick, positions, features, cotangent, uv, down)


def swap(value, axis):
    return lax.ppermute(value, axis, [(0, 1), (1, 0)])


def sum_scatter(value, axis):
    n = lax.axis_size(axis)
    parts = lax.all_to_all(value.reshape(n, value.shape[0] // n, 128), axis, 0, 0)
    return jnp.sum(parts, 0)


def gather(value, axis):
    n = lax.axis_size(axis)
    copies = jnp.broadcast_to(value[None], (n,) + value.shape)
    return lax.all_to_all(copies, axis, 0, 0).reshape(n * value.shape[0], 128)


def order_channels(own, across, beside, far, y_at, core_at):
    mine_y = jnp.where(y_at == 0, jnp.stack([own, across]), jnp.stack([across, own]))
    other_y = jnp.where(y_at == 0, jnp.stack([beside, far]), jnp.stack([far, beside]))
    even = jnp.where(core_at == 0, mine_y, other_y)
    odd = jnp.where(core_at == 0, other_y, mine_y)
    return jnp.concatenate([even[0], odd[0], even[1], odd[1]], 0).T


def shards(block, positions, features, cotangent, miller, radial_filter):
    atoms = positions.shape[1]
    waves = miller.shape[1]
    y_at, core_at = lax.axis_index("yl"), lax.axis_index("core")
    atom_count = atoms * lax.axis_size(("z", "yh", "x"))
    wave_count = waves * lax.axis_size(("yl", "core"))
    scale = float(atom_count * wave_count) ** (-0.5)
    pick = (2 * y_at + core_at).astype(jnp.int32).reshape(1)

    turned = radial_filter.T.reshape(2, 64, waves)
    indices = jnp.concatenate([miller.astype(f32), jnp.zeros((5, waves), f32)], 0)
    keep = jnp.where(y_at == 0, turned[0], turned[1])
    send = jnp.where(y_at == 0, turned[1], turned[0])
    here = jnp.concatenate([keep, indices], 0)
    there = swap(jnp.concatenate([send, indices], 0), "yl")
    pair = jnp.concatenate([here, there], 1)
    first, second, pair_indices = pair[:32], pair[32:64], pair[64:]
    keep = jnp.where(core_at == 0, first, second)
    send = jnp.where(core_at == 0, second, first)
    beside = swap(jnp.concatenate([send, pair_indices], 0), "core")
    radial_rows = jnp.concatenate([keep, beside[:32]], 1)
    miller_rows = jnp.concatenate([pair_indices, beside[32:]], 1)
    wave_block = min(1024, 4 * waves)
    classes = class_sums(miller_rows, radial_rows, wave_block)

    part = factors(pick, positions, features, cotangent, block)
    part = sum_scatter(part, "x")
    part = sum_scatter(part, "z")
    part = part + swap(part, "yh")
    part = gather(part, "z")
    total = gather(part, "x")
    uv, down, pair_products = combine(total, classes, scale)
    grad, posg = gradients(pick, positions, features, cotangent, uv, down, block)
    across = swap(grad, "yl")
    near = swap(jnp.concatenate([grad, across], 0), "core")
    feature_grad = order_channels(grad, across, near[:32], near[32:], y_at, core_at)
    posg = posg + swap(posg, "core")
    position_grad = posg + swap(posg, "yl")

    rows = filter_rows(miller_rows, pair_products, scale, wave_block).reshape(32, 4, waves)
    came = swap(rows[:, 1::2].reshape(32, 2 * waves), "yl").reshape(32, 2, waves)
    both = jnp.concatenate([rows[:, 0::2], came], 0)
    near = swap(both[:, 1], "core")
    filter_grad = order_channels(both[:32, 0], both[32:, 0], near[:32], near[32:], y_at, core_at)
    return feature_grad, position_grad, filter_grad


def solution(mesh):
    x, yh = 4, 2
    z = mesh.shape["atom"] // (x * yh)
    fine = Mesh(mesh.devices.reshape(z, yh, x, 2, 2), ("z", "yh", "x", "yl", "core"))
    atom, wave = ("z", "yh", "x"), ("yl", "core")
    placed = (P(None, atom), P(atom, None), P(atom, None), P(None, wave), P(wave, None))
    return jax.shard_map(
        functools.partial(shards, 512),
        mesh=fine,
        in_specs=placed,
        out_specs=(P(atom, None), P(None, atom), P(wave, None)),
        check_vma=False,
    )
```

```python
import functools
import math

import jax
import jax.numpy as jnp
from jax import lax
from jax.experimental import pallas as pl
from jax.experimental.pallas import tpu as pltpu
from jax.sharding import Mesh, PartitionSpec as P

phase_step = 2.0 * math.pi / 256.0
PAIRS = 296
PAIR_ROWS = 304
TILES = 9
SLOTS = 17 * 64
CLASSES = 896
PACKED = 2560
f32 = jnp.float32
bf16 = jnp.bfloat16
VMEM_LIMIT = 56 * 1024 * 1024


def nt_dot(a, b):
    return lax.dot_general(a, b, (((1,), (1,)), ((), ())), preferred_element_type=f32)


def turn_trig(turns):
    x = (turns - jnp.floor(turns + 0.5)) * (2.0 * math.pi)
    square = x * x
    cosine = jnp.full_like(x, 1.0 / math.factorial(18) * -1.0)
    for power in range(16, -1, -2):
        cosine = cosine * square + ((-1.0) ** (power // 2) / math.factorial(power))
    sine = jnp.full_like(x, 1.0 / math.factorial(17))
    for power in range(15, 0, -2):
        sine = sine * square + ((-1.0) ** (power // 2) / math.factorial(power))
    return cosine, sine * x


def multiples(position_rows):
    count = position_rows.shape[1]
    orders = lax.broadcasted_iota(jnp.int32, (8, count), 0).astype(f32) + 1.0
    return [turn_trig(orders * (position_rows[d : d + 1, :] * (1.0 / 256.0))) for d in range(3)]


def pair_table(trig1, trig2):
    (c1, s1), (c2, s2) = trig1, trig2
    count = c1.shape[1]
    tiles = []
    for left in (c1, s1):
        for right in (c2, s2):
            for m in range(8):
                tiles.append(left[m : m + 1, :] * right)
    one = (lax.broadcasted_iota(jnp.int32, (16, count), 0) == 0).astype(f32)
    tiles += [c2, s2, c1, s1, one]
    return jnp.concatenate(tiles, 0)


def row_tables(pick_ref, features, cotangent):
    lane = lax.broadcasted_iota(jnp.int32, (32, 128), 1)
    row = lax.broadcasted_iota(jnp.int32, (32, 128), 0)
    pick = (lane == row + 32 * pick_ref[0]).astype(bf16)
    return jnp.concatenate([nt_dot(pick, features), nt_dot(pick, cotangent)], 0)


def fill_slots(slots_ref, trig0, rows):
    c0, s0 = trig0
    for t in range(8):
        slots_ref[128 * t : 128 * t + 64, :] = (c0[t : t + 1, :] * rows).astype(bf16)
        slots_ref[128 * t + 64 : 128 * t + 128, :] = (s0[t : t + 1, :] * rows).astype(bf16)
    slots_ref[1024:1088, :] = rows.astype(bf16)


def factor_kernel(pick_ref, pos_ref, feat_ref, cot_ref, out_ref, total_ref, *slots_refs):
    step = pl.program_id(0)
    size = slots_refs[0].shape[1]
    product = None
    for k, slots_ref in enumerate(slots_refs):
        at = slice(k * size, (k + 1) * size)
        trig = multiples(pos_ref[:, at])
        fill_slots(slots_ref, trig[0], row_tables(pick_ref, feat_ref[at, :], cot_ref[at, :]))
        pairs = pair_table(trig[1], trig[2]).astype(bf16)
        part = nt_dot(pairs, slots_ref[...])
        product = part if product is None else product + part

    @pl.when(step == 0)
    def _():
        total_ref[...] = product

    @pl.when(step > 0)
    def _():
        total_ref[...] += product

    @pl.when(step == pl.num_programs(0) - 1)
    def _():
        for t in range(8):
            out_ref[PAIRS * t : PAIRS * (t + 1), :] = total_ref[0:PAIRS, 128 * t : 128 * t + 128]
        last = total_ref[:, 1024:1088]
        out_ref[2368:2520, :] = jnp.concatenate([last[0:152], last[152:304]], 1)
        out_ref[2520:2560, :] = jnp.zeros((40, 128), f32)


def factors(pick, positions, features, cotangent, block, cuts):
    atoms = positions.shape[1]
    return pl.pallas_call(
        factor_kernel,
        grid=(atoms // block,),
        in_specs=[
            pl.BlockSpec(memory_space=pltpu.SMEM),
            pl.BlockSpec((3, block), lambda i: (0, i)),
            pl.BlockSpec((block, 128), lambda i: (i, 0)),
            pl.BlockSpec((block, 128), lambda i: (i, 0)),
        ],
        out_specs=pl.BlockSpec((PACKED, 128), lambda i: (0, 0)),
        out_shape=jax.ShapeDtypeStruct((PACKED, 128), f32),
        scratch_shapes=[pltpu.VMEM((PAIR_ROWS, SLOTS), f32)] + [pltpu.VMEM((SLOTS, block // cuts), bf16)] * cuts,
        compiler_params=pltpu.CompilerParams(vmem_limit_bytes=VMEM_LIMIT),
        cost_estimate=pl.CostEstimate(flops=2 * PAIR_ROWS * SLOTS * atoms, bytes_accessed=atoms * 520, transcendentals=0),
        name="factors",
    )(pick, positions, features, cotangent)


def wave_class(m):
    m0, m1, m2 = [m[d : d + 1, :] for d in range(3)]
    size0, size1, size2 = jnp.abs(m0), jnp.abs(m1), jnp.abs(m2)
    signs = [jnp.clip(v, -1.0, 1.0) for v in (m0, m1, m2)]
    both = (size1 - 1.0) * 8.0 + size2 - 1.0
    inner = jnp.where(
        size1 > 0.0,
        jnp.where(size2 > 0.0, both, 72.0 + size1 - 1.0),
        jnp.where(size2 > 0.0, 64.0 + size2 - 1.0, 80.0),
    )
    tile = jnp.where(size0 > 0.0, size0 - 1.0, 8.0)
    index = (tile * 88.0 + inner).astype(jnp.int32)
    return index, (signs[1] * signs[2], signs[0] * signs[1], signs[0] * signs[2])


def split_hi_lo(v):
    hi = v.astype(bf16)
    return hi, (v - hi.astype(f32)).astype(bf16)


def class_kernel(scale, miller_ref, radial_ref, out_ref, sum_ref):
    step = pl.program_id(0)
    index, products = wave_class(miller_ref[0:3, :])
    radial = radial_ref[...]
    signed = jnp.concatenate([radial] + [radial * p for p in products], 0)
    hi, lo = split_hi_lo(signed)
    hot = (lax.broadcasted_iota(jnp.int32, (CLASSES, index.shape[1]), 0) == index).astype(f32).astype(bf16)
    part = nt_dot(hot, jnp.concatenate([hi, lo], 0))
    part = part[:, :128] + part[:, 128:]

    @pl.when(step == 0)
    def _():
        sum_ref[...] = part

    @pl.when(step > 0)
    def _():
        sum_ref[...] += part

    @pl.when(step == pl.num_programs(0) - 1)
    def _():
        for q in range(4):
            one = sum_ref[:, 32 * q : 32 * q + 32] * scale
            out_ref[q] = jnp.concatenate([one, one, one, one], 1)


def class_sums(miller_rows, radial_rows, scale, block):
    waves = miller_rows.shape[1]
    return pl.pallas_call(
        functools.partial(class_kernel, scale),
        grid=(waves // block,),
        in_specs=[pl.BlockSpec((8, block), lambda i: (0, i)), pl.BlockSpec((32, block), lambda i: (0, i))],
        out_specs=pl.BlockSpec((4, CLASSES, 128), lambda i: (0, 0, 0)),
        out_shape=jax.ShapeDtypeStruct((4, CLASSES, 128), f32),
        scratch_shapes=[pltpu.VMEM((CLASSES, 128), f32)],
        compiler_params=pltpu.CompilerParams(vmem_limit_bytes=VMEM_LIMIT),
        cost_estimate=pl.CostEstimate(flops=2 * CLASSES * 256 * waves, bytes_accessed=waves * 160, transcendentals=0),
        name="class_sums",
    )(miller_rows, radial_rows)


def load_tile(total_ref, t):
    if t < 8:
        return total_ref[PAIRS * t : PAIRS * (t + 1), :]
    fold = total_ref[2368:2520, :]
    last = jnp.concatenate([fold[:, :64], fold[0:144, 64:]], 0)
    return jnp.concatenate([last, jnp.zeros((PAIRS, 64), f32)], 1)


def lane_signs():
    lane = lax.broadcasted_iota(jnp.int32, (1, 128), 1)
    return lane, jnp.where(lane < 64, 1.0, -1.0).astype(f32)


def cut(v):
    return [v[0:64], v[64:128], v[128:192], v[192:256]] + [v[256 + 8 * k : 264 + 8 * k] for k in range(5)]


def combine(total_ref, class_ref, uv_ref, down_ref):
    lane, half = lane_signs()
    swap = (lane % 64) < 32
    pick_lane = lax.broadcasted_iota(jnp.int32, (64, 128), 1)
    pick_row = lax.broadcasted_iota(jnp.int32, (64, 128), 0)
    pick = (pick_lane == jnp.where(pick_row < 32, pick_row + 32, pick_row + 64)).astype(bf16)
    for t in range(TILES):
        a = load_tile(total_ref, t)
        x0, x1, x2, x3 = [class_ref[q, 88 * t : 88 * t + 88, :] for q in range(4)]
        i0, i1, i2, i3 = [v[0:64] for v in (x0, x1, x2, x3)]
        cc, cs, sc, ss, e2c, e2s, e1c, e1s, co = cut(a)
        f0, f3 = x0[64:72], x3[64:72]
        g0, g2 = x0[72:80], x2[72:80]
        if t < 8:
            bcc, bcs, bsc, bss, be2c, be2s, be1c, be1s, _ = cut(half * pltpu.roll(a, 64, 1))
            blocks = [
                i0 * cc - i1 * ss - i2 * bsc - i3 * bcs,
                i0 * cs + i1 * sc - i2 * bss + i3 * bcc,
                i0 * sc + i1 * cs + i2 * bcc - i3 * bss,
                i0 * ss - i1 * cc + i2 * bcs + i3 * bsc,
                f0 * e2c - f3 * be2s,
                f0 * e2s + f3 * be2c,
                g0 * e1c - g2 * be1s,
                g0 * e1s + g2 * be1c,
            ]
        else:
            blocks = [i0 * cc - i1 * ss, i0 * cs + i1 * sc, i0 * sc + i1 * cs, i0 * ss - i1 * cc]
            blocks += [f0 * e2c, f0 * e2s, g0 * e1c, g0 * e1s]
        w = jnp.concatenate(blocks + [x0[80:88] * co, jnp.zeros((8, 128), f32)], 0)
        swapped = jnp.where(swap, pltpu.roll(w, 96, 1), pltpu.roll(w, 32, 1))
        uv_ref[0:PAIR_ROWS, 128 * t : 128 * t + 128] = swapped.astype(bf16)
        if t < 8:
            slope = (t + 1.0) * half * pltpu.roll(swapped, 64, 1)
        else:
            slope = jnp.zeros((PAIR_ROWS, 128), f32)
        uv_ref[PAIR_ROWS : 2 * PAIR_ROWS, 128 * t : 128 * t + 128] = slope.astype(bf16)
        down_ref[64 * t : 64 * t + 64, :] = nt_dot(pick, w.astype(bf16)).astype(bf16)


def pair_products(total_ref, pair_ref):
    _, half = lane_signs()
    pair_ref[...] = jnp.zeros((CLASSES, 128), f32)
    for t in range(TILES):
        a = load_tile(total_ref, t)
        b = half * pltpu.roll(a, 64, 1)
        sa = pltpu.roll(a, 32, 1)
        sb = pltpu.roll(b, 32, 1)
        cc, cs, sc, ss, e2c, e2s, e1c, e1s, co = cut(a)
        scc, scs, ssc, sss, se2c, se2s, se1c, se1s, sco = cut(sa)
        tcc, tcs, tsc, tss, te2c, te2s, te1c, te1s, _ = cut(sb)
        zero = jnp.zeros((8, 128), f32)
        y = [
            [cc * scc + cs * scs + sc * ssc + ss * sss, e2c * se2c + e2s * se2s, e1c * se1c + e1s * se1s, co * sco],
            [cs * ssc + sc * scs - cc * sss - ss * scc, zero, zero, zero],
            [sc * tcc + ss * tcs - cc * tsc - cs * tss, zero, e1s * te1c - e1c * te1s, zero],
            [cs * tcc + ss * tsc - cc * tcs - sc * tss, e2s * te2c - e2c * te2s, zero, zero],
        ]
        parts = []
        for q in range(4):
            z = jnp.concatenate(y[q], 0)
            parts.append(z[:, 32:64] + z[:, 96:128])
        pair_ref[88 * t : 88 * t + 88, :] = jnp.concatenate(parts, 1)


def filter_kernel(scale, miller_ref, total_ref, own_ref, beside_ref, send_ref, pair_ref, turned_ref):
    step = pl.program_id(0)

    @pl.when(step == 0)
    def _():
        pair_products(total_ref, pair_ref)
        hi, lo = split_hi_lo(pair_ref[...].T)
        turned_ref[0:128, :] = hi
        turned_ref[128:256, :] = lo

    index, products = wave_class(miller_ref[0:3, :])
    hot = (lax.broadcasted_iota(jnp.int32, (CLASSES, index.shape[1]), 0) == index).astype(f32).astype(bf16)
    values = jnp.dot(turned_ref[...], hot, preferred_element_type=f32)
    values = values[:128] + values[128:]
    rows = values[0:32]
    for q in range(3):
        rows = rows + products[q] * values[32 * (q + 1) : 32 * (q + 2)]
    rows = scale * rows

    @pl.when(step == 0)
    def _():
        own_ref[...] = rows

    @pl.when(step == 2)
    def _():
        beside_ref[...] = rows

    @pl.when(lax.rem(step, 2) == 1)
    def _():
        send_ref[0] = rows


def filter_rows(miller_rows, total, scale):
    block = miller_rows.shape[1] // 4
    one = jax.ShapeDtypeStruct((32, block), f32)
    return pl.pallas_call(
        functools.partial(filter_kernel, scale),
        grid=(4,),
        in_specs=[pl.BlockSpec((8, block), lambda i: (0, i)), pl.BlockSpec((PACKED, 128), lambda i: (0, 0))],
        out_specs=(
            pl.BlockSpec((32, block), lambda i: (0, 0)),
            pl.BlockSpec((32, block), lambda i: (0, 0)),
            pl.BlockSpec((1, 32, block), lambda i: (i // 2, 0, 0)),
        ),
        out_shape=(one, one, jax.ShapeDtypeStruct((2, 32, block), f32)),
        scratch_shapes=[pltpu.VMEM((CLASSES, 128), f32), pltpu.VMEM((256, CLASSES), bf16)],
        compiler_params=pltpu.CompilerParams(vmem_limit_bytes=VMEM_LIMIT),
        cost_estimate=pl.CostEstimate(flops=2 * CLASSES * 1024 * block, bytes_accessed=block * 640, transcendentals=0),
        name="filter_rows",
    )(miller_rows, total)


def feature_kernel(pos_ref, total_ref, class_ref, grad_ref, uv_ref, down_ref):
    @pl.when(pl.program_id(0) == 0)
    def _():
        combine(total_ref, class_ref, uv_ref, down_ref)

    (c0, s0), trig1, trig2 = multiples(pos_ref[...])
    pairs = pair_table(trig1, trig2).astype(bf16)
    parts = jnp.dot(down_ref[...], pairs, preferred_element_type=f32)
    grad = parts[512:544]
    for t in range(8):
        grad = grad + c0[t : t + 1, :] * parts[64 * t : 64 * t + 32] + s0[t : t + 1, :] * parts[64 * t + 32 : 64 * t + 64]
    grad_ref[...] = grad


def feature_rows(positions, total, classes, block):
    atoms = positions.shape[1]
    return pl.pallas_call(
        feature_kernel,
        grid=(atoms // block,),
        in_specs=[
            pl.BlockSpec((3, block), lambda i: (0, i)),
            pl.BlockSpec((PACKED, 128), lambda i: (0, 0)),
            pl.BlockSpec((4, CLASSES, 128), lambda i: (0, 0, 0)),
        ],
        out_specs=(
            pl.BlockSpec((32, block), lambda i: (0, i)),
            pl.BlockSpec((2 * PAIR_ROWS, 128 * TILES), lambda i: (0, 0)),
        ),
        out_shape=(
            jax.ShapeDtypeStruct((32, atoms), f32),
            jax.ShapeDtypeStruct((2 * PAIR_ROWS, 128 * TILES), bf16),
        ),
        scratch_shapes=[pltpu.VMEM((64 * TILES, PAIR_ROWS), bf16)],
        compiler_params=pltpu.CompilerParams(vmem_limit_bytes=VMEM_LIMIT),
        cost_estimate=pl.CostEstimate(flops=2 * PAIR_ROWS * SLOTS * atoms, bytes_accessed=atoms * 700, transcendentals=0),
        name="feature_rows",
    )(positions, total, classes)


def position_kernel(pick_ref, pos_ref, feat_ref, cot_ref, uv_ref, posg_ref, *slots_refs):
    size = slots_refs[0].shape[1]
    for k, slots_ref in enumerate(slots_refs):
        at = slice(k * size, (k + 1) * size)
        trig = multiples(pos_ref[:, at])
        fill_slots(slots_ref, trig[0], row_tables(pick_ref, feat_ref[at, :], cot_ref[at, :]))
        both = jnp.dot(uv_ref[:, 0:SLOTS], slots_ref[...], preferred_element_type=f32)
        posg_ref[:, at] = position_sums(trig, both[0:PAIR_ROWS], both[PAIR_ROWS:])


def position_sums(trig, u, v):
    _, (c1, s1), (c2, s2) = trig
    orders = lax.broadcasted_iota(jnp.int32, c1.shape, 0).astype(f32) + 1.0
    acc0 = c2 * v[256:264] + s2 * v[264:272] + c1 * v[272:280] + s1 * v[280:288]
    acc1 = orders * (c1 * u[280:288] - s1 * u[272:280])
    acc2 = c2 * u[264:272] - s2 * u[256:264]
    for m in range(8):
        lead_c, lead_s = c1[m : m + 1, :], s1[m : m + 1, :]
        ucc, ucs, usc, uss = [u[64 * k + 8 * m : 64 * k + 8 * m + 8] for k in range(4)]
        vcc, vcs, vsc, vss = [v[64 * k + 8 * m : 64 * k + 8 * m + 8] for k in range(4)]
        acc0 = acc0 + lead_c * (c2 * vcc + s2 * vcs) + lead_s * (c2 * vsc + s2 * vss)
        acc1 = acc1 + float(m + 1) * (lead_c * (c2 * usc + s2 * uss) - lead_s * (c2 * ucc + s2 * ucs))
        acc2 = acc2 + lead_c * (c2 * ucs - s2 * ucc) + lead_s * (c2 * uss - s2 * usc)
    acc2 = acc2 * orders
    rows = [jnp.sum(acc0, 0, keepdims=True) + v[288:289], jnp.sum(acc1, 0, keepdims=True), jnp.sum(acc2, 0, keepdims=True)]
    return phase_step * jnp.concatenate(rows, 0)


def position_rows(pick, positions, features, cotangent, uv, block, cuts):
    atoms = positions.shape[1]
    return pl.pallas_call(
        position_kernel,
        grid=(atoms // block,),
        in_specs=[
            pl.BlockSpec(memory_space=pltpu.SMEM),
            pl.BlockSpec((3, block), lambda i: (0, i)),
            pl.BlockSpec((block, 128), lambda i: (i, 0)),
            pl.BlockSpec((block, 128), lambda i: (i, 0)),
            pl.BlockSpec((2 * PAIR_ROWS, 128 * TILES), lambda i: (0, 0)),
        ],
        out_specs=pl.BlockSpec((3, block), lambda i: (0, i)),
        out_shape=jax.ShapeDtypeStruct((3, atoms), f32),
        scratch_shapes=[pltpu.VMEM((SLOTS, block // cuts), bf16)] * cuts,
        compiler_params=pltpu.CompilerParams(vmem_limit_bytes=VMEM_LIMIT),
        cost_estimate=pl.CostEstimate(flops=4 * PAIR_ROWS * SLOTS * atoms, bytes_accessed=atoms * 700, transcendentals=0),
        name="position_rows",
    )(pick, positions, features, cotangent, uv)


def swap(value, axis):
    return lax.ppermute(value, axis, [(0, 1), (1, 0)])


def sum_scatter(value, axis):
    n = lax.axis_size(axis)
    parts = lax.all_to_all(value.reshape(n, value.shape[0] // n, 128), axis, 0, 0)
    return jnp.sum(parts, 0)


def gather(value, axis):
    n = lax.axis_size(axis)
    copies = jnp.broadcast_to(value[None], (n,) + value.shape)
    return lax.all_to_all(copies, axis, 0, 0).reshape(n * value.shape[0], 128)


def order_channels(own, across, beside, far, y_at, core_at):
    mine_y = jnp.where(y_at == 0, jnp.stack([own, across]), jnp.stack([across, own]))
    other_y = jnp.where(y_at == 0, jnp.stack([beside, far]), jnp.stack([far, beside]))
    even = jnp.where(core_at == 0, mine_y, other_y)
    odd = jnp.where(core_at == 0, other_y, mine_y)
    return jnp.concatenate([even[0], odd[0], even[1], odd[1]], 0).T


def shards(block, positions, features, cotangent, miller, radial_filter):
    atoms = positions.shape[1]
    block = min(block, atoms)
    waves = miller.shape[1]
    y_at, core_at = lax.axis_index("yl"), lax.axis_index("core")
    atom_count = atoms * lax.axis_size(("z", "yh", "x"))
    wave_count = waves * lax.axis_size(("yl", "core"))
    scale = float(atom_count * wave_count) ** (-0.5)
    pick = (2 * y_at + core_at).astype(jnp.int32).reshape(1)

    turned = radial_filter.T.reshape(2, 64, waves)
    indices = jnp.concatenate([miller.astype(f32), jnp.zeros((5, waves), f32)], 0)
    keep = jnp.where(y_at == 0, turned[0], turned[1])
    send = jnp.where(y_at == 0, turned[1], turned[0])
    here = jnp.concatenate([keep, indices], 0)
    there = swap(jnp.concatenate([send, indices], 0), "yl")
    pair = jnp.concatenate([here, there], 1)
    first, second, pair_indices = pair[:32], pair[32:64], pair[64:]
    keep = jnp.where(core_at == 0, first, second)
    send = jnp.where(core_at == 0, second, first)
    beside = swap(jnp.concatenate([send, pair_indices], 0), "core")
    radial_rows = jnp.concatenate([keep, beside[:32]], 1)
    miller_rows = jnp.concatenate([pair_indices, beside[32:]], 1)
    classes = class_sums(miller_rows, radial_rows, scale, min(1024, 4 * waves))

    part = factors(pick, positions, features, cotangent, block, 1)
    part = sum_scatter(part, ("x", "yh"))
    part = sum_scatter(part, "z")
    part = gather(part, "z")
    total = gather(part, ("x", "yh"))
    grad, uv = feature_rows(positions, total, classes, atoms)
    grad_y, grad_core = swap(grad, "yl"), swap(grad, "core")
    total = lax.optimization_barrier((total, grad))[0]
    own, beside, send = filter_rows(miller_rows, total, scale)
    came, beside = swap(send, "yl"), swap(beside, "core")
    uv = lax.optimization_barrier((uv, own))[0]
    posg = position_rows(pick, positions, features, cotangent, uv, block, 1)
    grad_y, came, posg = lax.optimization_barrier((grad_y, came, posg))
    both = lax.ppermute(posg, ("yl", "core"), [(i, 3 - i) for i in range(4)])
    position_grad = (posg + swap(posg, "core")) + (swap(posg, "yl") + both)
    feature_grad = order_channels(grad, grad_y, grad_core, swap(grad_y, "core"), y_at, core_at)
    filter_grad = order_channels(own, came[0], beside, swap(came, "core")[1], y_at, core_at)
    return feature_grad, position_grad, filter_grad


def solution(mesh):
    x, yh = 4, 2
    z = mesh.shape["atom"] // (x * yh)
    fine = Mesh(mesh.devices.reshape(z, yh, x, 2, 2), ("z", "yh", "x", "yl", "core"))
    atom, wave = ("z", "yh", "x"), ("yl", "core")
    placed = (P(None, atom), P(atom, None), P(atom, None), P(None, wave), P(wave, None))
    return jax.shard_map(
        functools.partial(shards, 2048),
        mesh=fine,
        in_specs=placed,
        out_specs=(P(atom, None), P(None, atom), P(wave, None)),
        check_vma=False,
    )
```

```python
import functools
import math

import jax
import jax.numpy as jnp
from jax import lax
from jax.experimental import pallas as pl
from jax.experimental.pallas import tpu as pltpu
from jax.sharding import Mesh, PartitionSpec as P

phase_step = 2.0 * math.pi / 256.0
PAIRS = 296
PAIR_ROWS = 304
TILES = 9
SLOTS = 17 * 64
CLASSES = 896
PACKED = 2560
f32 = jnp.float32
bf16 = jnp.bfloat16
MIB = 1024 * 1024


def nt_dot(a, b):
    return lax.dot_general(a, b, (((1,), (1,)), ((), ())), preferred_element_type=f32)


def turn_trig(turns):
    x = (turns - jnp.floor(turns + 0.5)) * (2.0 * math.pi)
    square = x * x
    cosine = jnp.full_like(x, 1.0 / math.factorial(18) * -1.0)
    for power in range(16, -1, -2):
        cosine = cosine * square + ((-1.0) ** (power // 2) / math.factorial(power))
    sine = jnp.full_like(x, 1.0 / math.factorial(17))
    for power in range(15, 0, -2):
        sine = sine * square + ((-1.0) ** (power // 2) / math.factorial(power))
    return cosine, sine * x


def multiples(position_rows):
    count = position_rows.shape[1]
    orders = lax.broadcasted_iota(jnp.int32, (8, count), 0).astype(f32) + 1.0
    return [turn_trig(orders * (position_rows[d : d + 1, :] * (1.0 / 256.0))) for d in range(3)]


def pair_table(trig1, trig2):
    (c1, s1), (c2, s2) = trig1, trig2
    count = c1.shape[1]
    tiles = []
    for left in (c1, s1):
        for right in (c2, s2):
            for m in range(8):
                tiles.append(left[m : m + 1, :] * right)
    one = (lax.broadcasted_iota(jnp.int32, (16, count), 0) == 0).astype(f32)
    tiles += [c2, s2, c1, s1, one]
    return jnp.concatenate(tiles, 0)


def row_tables(pick_ref, features, cotangent):
    lane = lax.broadcasted_iota(jnp.int32, (32, 128), 1)
    row = lax.broadcasted_iota(jnp.int32, (32, 128), 0)
    pick = (lane == row + 32 * pick_ref[0]).astype(bf16)
    return jnp.concatenate([nt_dot(pick, features), nt_dot(pick, cotangent)], 0)


def fill_slots(slots_ref, trig0, rows):
    c0, s0 = trig0
    for t in range(8):
        slots_ref[128 * t : 128 * t + 64, :] = (c0[t : t + 1, :] * rows).astype(bf16)
        slots_ref[128 * t + 64 : 128 * t + 128, :] = (s0[t : t + 1, :] * rows).astype(bf16)
    slots_ref[1024:1088, :] = rows.astype(bf16)


def factor_kernel(pick_ref, pos_ref, feat_ref, cot_ref, out_ref, total_ref, *slots_refs):
    step = pl.program_id(0)
    size = slots_refs[0].shape[1]
    product = None
    for k, slots_ref in enumerate(slots_refs):
        at = slice(k * size, (k + 1) * size)
        trig = multiples(pos_ref[:, at])
        fill_slots(slots_ref, trig[0], row_tables(pick_ref, feat_ref[at, :], cot_ref[at, :]))
        pairs = pair_table(trig[1], trig[2]).astype(bf16)
        part = nt_dot(pairs, slots_ref[...])
        product = part if product is None else product + part

    @pl.when(step == 0)
    def _():
        total_ref[...] = product

    @pl.when(step > 0)
    def _():
        total_ref[...] += product

    @pl.when(step == pl.num_programs(0) - 1)
    def _():
        for t in range(8):
            out_ref[PAIRS * t : PAIRS * (t + 1), :] = total_ref[0:PAIRS, 128 * t : 128 * t + 128]
        last = total_ref[:, 1024:1088]
        out_ref[2368:2520, :] = jnp.concatenate([last[0:152], last[152:304]], 1)
        out_ref[2520:2560, :] = jnp.zeros((40, 128), f32)


def factors(pick, positions, features, cotangent, block, cuts):
    atoms = positions.shape[1]
    return pl.pallas_call(
        factor_kernel,
        grid=(atoms // block,),
        in_specs=[
            pl.BlockSpec(memory_space=pltpu.SMEM),
            pl.BlockSpec((3, block), lambda i: (0, i)),
            pl.BlockSpec((block, 128), lambda i: (i, 0)),
            pl.BlockSpec((block, 128), lambda i: (i, 0)),
        ],
        out_specs=pl.BlockSpec((PACKED, 128), lambda i: (0, 0)),
        out_shape=jax.ShapeDtypeStruct((PACKED, 128), f32),
        scratch_shapes=[pltpu.VMEM((PAIR_ROWS, SLOTS), f32)] + [pltpu.VMEM((SLOTS, block // cuts), bf16)] * cuts,
        compiler_params=pltpu.CompilerParams(vmem_limit_bytes=56 * MIB),
        cost_estimate=pl.CostEstimate(flops=2 * PAIR_ROWS * SLOTS * atoms, bytes_accessed=atoms * 520, transcendentals=0),
        name="factors",
    )(pick, positions, features, cotangent)


def wave_class(m):
    m0, m1, m2 = [m[d : d + 1, :] for d in range(3)]
    size0, size1, size2 = jnp.abs(m0), jnp.abs(m1), jnp.abs(m2)
    signs = [jnp.clip(v, -1.0, 1.0) for v in (m0, m1, m2)]
    both = (size1 - 1.0) * 8.0 + size2 - 1.0
    inner = jnp.where(
        size1 > 0.0,
        jnp.where(size2 > 0.0, both, 72.0 + size1 - 1.0),
        jnp.where(size2 > 0.0, 64.0 + size2 - 1.0, 80.0),
    )
    tile = jnp.where(size0 > 0.0, size0 - 1.0, 8.0)
    index = (tile * 88.0 + inner).astype(jnp.int32)
    return index, (signs[1] * signs[2], signs[0] * signs[1], signs[0] * signs[2])


def split_hi_lo(v):
    hi = v.astype(bf16)
    return hi, (v - hi.astype(f32)).astype(bf16)


def class_kernel(scale, miller_ref, radial_ref, out_ref, sum_ref):
    step = pl.program_id(0)
    index, products = wave_class(miller_ref[0:3, :])
    radial = radial_ref[...]
    signed = jnp.concatenate([radial] + [radial * p for p in products], 0)
    hi, lo = split_hi_lo(signed)
    hot = (lax.broadcasted_iota(jnp.int32, (CLASSES, index.shape[1]), 0) == index).astype(f32).astype(bf16)
    part = nt_dot(hot, jnp.concatenate([hi, lo], 0))
    part = part[:, :128] + part[:, 128:]

    @pl.when(step == 0)
    def _():
        sum_ref[...] = part

    @pl.when(step > 0)
    def _():
        sum_ref[...] += part

    @pl.when(step == pl.num_programs(0) - 1)
    def _():
        for q in range(4):
            one = sum_ref[:, 32 * q : 32 * q + 32] * scale
            out_ref[q] = jnp.concatenate([one, one, one, one], 1)


def class_sums(miller_rows, radial_rows, scale, block):
    waves = miller_rows.shape[1]
    return pl.pallas_call(
        functools.partial(class_kernel, scale),
        grid=(waves // block,),
        in_specs=[pl.BlockSpec((8, block), lambda i: (0, i)), pl.BlockSpec((32, block), lambda i: (0, i))],
        out_specs=pl.BlockSpec((4, CLASSES, 128), lambda i: (0, 0, 0)),
        out_shape=jax.ShapeDtypeStruct((4, CLASSES, 128), f32),
        scratch_shapes=[pltpu.VMEM((CLASSES, 128), f32)],
        compiler_params=pltpu.CompilerParams(vmem_limit_bytes=18 * MIB),
        cost_estimate=pl.CostEstimate(flops=2 * CLASSES * 256 * waves, bytes_accessed=waves * 160, transcendentals=0),
        name="class_sums",
    )(miller_rows, radial_rows)


def load_tile(total_ref, t):
    if t < 8:
        return total_ref[PAIRS * t : PAIRS * (t + 1), :]
    fold = total_ref[2368:2520, :]
    last = jnp.concatenate([fold[:, :64], fold[0:144, 64:]], 0)
    return jnp.concatenate([last, jnp.zeros((PAIRS, 64), f32)], 1)


def lane_signs():
    lane = lax.broadcasted_iota(jnp.int32, (1, 128), 1)
    return lane, jnp.where(lane < 64, 1.0, -1.0).astype(f32)


def cut(v):
    return [v[0:64], v[64:128], v[128:192], v[192:256]] + [v[256 + 8 * k : 264 + 8 * k] for k in range(5)]


def combine(total_ref, class_ref, uv_ref, down_ref):
    lane, half = lane_signs()
    swap = (lane % 64) < 32
    pick_lane = lax.broadcasted_iota(jnp.int32, (64, 128), 1)
    pick_row = lax.broadcasted_iota(jnp.int32, (64, 128), 0)
    pick = (pick_lane == jnp.where(pick_row < 32, pick_row + 32, pick_row + 64)).astype(bf16)
    for t in range(TILES):
        a = load_tile(total_ref, t)
        x0, x1, x2, x3 = [class_ref[q, 88 * t : 88 * t + 88, :] for q in range(4)]
        i0, i1, i2, i3 = [v[0:64] for v in (x0, x1, x2, x3)]
        cc, cs, sc, ss, e2c, e2s, e1c, e1s, co = cut(a)
        f0, f3 = x0[64:72], x3[64:72]
        g0, g2 = x0[72:80], x2[72:80]
        if t < 8:
            bcc, bcs, bsc, bss, be2c, be2s, be1c, be1s, _ = cut(half * pltpu.roll(a, 64, 1))
            blocks = [
                i0 * cc - i1 * ss - i2 * bsc - i3 * bcs,
                i0 * cs + i1 * sc - i2 * bss + i3 * bcc,
                i0 * sc + i1 * cs + i2 * bcc - i3 * bss,
                i0 * ss - i1 * cc + i2 * bcs + i3 * bsc,
                f0 * e2c - f3 * be2s,
                f0 * e2s + f3 * be2c,
                g0 * e1c - g2 * be1s,
                g0 * e1s + g2 * be1c,
            ]
        else:
            blocks = [i0 * cc - i1 * ss, i0 * cs + i1 * sc, i0 * sc + i1 * cs, i0 * ss - i1 * cc]
            blocks += [f0 * e2c, f0 * e2s, g0 * e1c, g0 * e1s]
        w = jnp.concatenate(blocks + [x0[80:88] * co, jnp.zeros((8, 128), f32)], 0)
        swapped = jnp.where(swap, pltpu.roll(w, 96, 1), pltpu.roll(w, 32, 1))
        uv_ref[0:PAIR_ROWS, 128 * t : 128 * t + 128] = swapped.astype(bf16)
        if t < 8:
            slope = (t + 1.0) * half * pltpu.roll(swapped, 64, 1)
        else:
            slope = jnp.zeros((PAIR_ROWS, 128), f32)
        uv_ref[PAIR_ROWS : 2 * PAIR_ROWS, 128 * t : 128 * t + 128] = slope.astype(bf16)
        down_ref[64 * t : 64 * t + 64, :] = nt_dot(pick, w.astype(bf16)).astype(bf16)


def pair_products(total_ref, pair_ref):
    _, half = lane_signs()
    pair_ref[...] = jnp.zeros((CLASSES, 128), f32)
    for t in range(TILES):
        a = load_tile(total_ref, t)
        b = half * pltpu.roll(a, 64, 1)
        sa = pltpu.roll(a, 32, 1)
        sb = pltpu.roll(b, 32, 1)
        cc, cs, sc, ss, e2c, e2s, e1c, e1s, co = cut(a)
        scc, scs, ssc, sss, se2c, se2s, se1c, se1s, sco = cut(sa)
        tcc, tcs, tsc, tss, te2c, te2s, te1c, te1s, _ = cut(sb)
        zero = jnp.zeros((8, 128), f32)
        y = [
            [cc * scc + cs * scs + sc * ssc + ss * sss, e2c * se2c + e2s * se2s, e1c * se1c + e1s * se1s, co * sco],
            [cs * ssc + sc * scs - cc * sss - ss * scc, zero, zero, zero],
            [sc * tcc + ss * tcs - cc * tsc - cs * tss, zero, e1s * te1c - e1c * te1s, zero],
            [cs * tcc + ss * tsc - cc * tcs - sc * tss, e2s * te2c - e2c * te2s, zero, zero],
        ]
        parts = []
        for q in range(4):
            z = jnp.concatenate(y[q], 0)
            parts.append(z[:, 32:64] + z[:, 96:128])
        pair_ref[88 * t : 88 * t + 88, :] = jnp.concatenate(parts, 1)


def filter_kernel(scale, miller_ref, total_ref, *refs):
    *out_refs, pair_ref, turned_ref = refs
    step = pl.program_id(0)

    @pl.when(step == 0)
    def _():
        pair_products(total_ref, pair_ref)
        hi, lo = split_hi_lo(pair_ref[...].T)
        turned_ref[0:128, :] = hi
        turned_ref[128:256, :] = lo

    index, products = wave_class(miller_ref[0:3, :])
    hot = (lax.broadcasted_iota(jnp.int32, (CLASSES, index.shape[1]), 0) == index).astype(f32).astype(bf16)
    values = jnp.dot(turned_ref[...], hot, preferred_element_type=f32)
    values = values[:128] + values[128:]
    rows = values[0:32]
    for q in range(3):
        rows = rows + products[q] * values[32 * (q + 1) : 32 * (q + 2)]
    rows = scale * rows

    for k, out_ref in enumerate(out_refs):

        @pl.when(step == k)
        def _():
            out_ref[...] = rows


def filter_rows(miller_rows, total, scale):
    block = miller_rows.shape[1] // 4
    one = jax.ShapeDtypeStruct((32, block), f32)
    return pl.pallas_call(
        functools.partial(filter_kernel, scale),
        grid=(4,),
        in_specs=[pl.BlockSpec((8, block), lambda i: (0, i)), pl.BlockSpec((PACKED, 128), lambda i: (0, 0))],
        out_specs=(pl.BlockSpec((32, block), lambda i: (0, 0)),) * 4,
        out_shape=(one,) * 4,
        scratch_shapes=[pltpu.VMEM((CLASSES, 128), f32), pltpu.VMEM((256, CLASSES), bf16)],
        compiler_params=pltpu.CompilerParams(vmem_limit_bytes=18 * MIB),
        cost_estimate=pl.CostEstimate(flops=2 * CLASSES * 1024 * block, bytes_accessed=block * 640, transcendentals=0),
        name="filter_rows",
    )(miller_rows, total)


def feature_kernel(pos_ref, total_ref, class_ref, grad_ref, uv_ref, down_ref):
    @pl.when(pl.program_id(0) == 0)
    def _():
        combine(total_ref, class_ref, uv_ref, down_ref)

    (c0, s0), trig1, trig2 = multiples(pos_ref[...])
    pairs = pair_table(trig1, trig2).astype(bf16)
    parts = jnp.dot(down_ref[...], pairs, preferred_element_type=f32)
    grad = parts[512:544]
    for t in range(8):
        grad = grad + c0[t : t + 1, :] * parts[64 * t : 64 * t + 32] + s0[t : t + 1, :] * parts[64 * t + 32 : 64 * t + 64]
    grad_ref[...] = grad


def feature_rows(positions, total, classes, block):
    atoms = positions.shape[1]
    return pl.pallas_call(
        feature_kernel,
        grid=(atoms // block,),
        in_specs=[
            pl.BlockSpec((3, block), lambda i: (0, i)),
            pl.BlockSpec((PACKED, 128), lambda i: (0, 0)),
            pl.BlockSpec((4, CLASSES, 128), lambda i: (0, 0, 0)),
        ],
        out_specs=(
            pl.BlockSpec((32, block), lambda i: (0, i)),
            pl.BlockSpec((2 * PAIR_ROWS, 128 * TILES), lambda i: (0, 0)),
        ),
        out_shape=(
            jax.ShapeDtypeStruct((32, atoms), f32),
            jax.ShapeDtypeStruct((2 * PAIR_ROWS, 128 * TILES), bf16),
        ),
        scratch_shapes=[pltpu.VMEM((64 * TILES, PAIR_ROWS), bf16)],
        compiler_params=pltpu.CompilerParams(vmem_limit_bytes=38 * MIB),
        cost_estimate=pl.CostEstimate(flops=2 * PAIR_ROWS * SLOTS * atoms, bytes_accessed=atoms * 700, transcendentals=0),
        name="feature_rows",
    )(positions, total, classes)


def position_half(pick_ref, pos_ref, feat_ref, cot_ref, uv_ref, slots_ref):
    trig = multiples(pos_ref[...])
    fill_slots(slots_ref, trig[0], row_tables(pick_ref, feat_ref[...], cot_ref[...]))
    both = jnp.dot(uv_ref[:, 0:1024], slots_ref[0:1024, :], preferred_element_type=f32)
    last = jnp.dot(uv_ref[0:PAIR_ROWS, 1024:SLOTS], slots_ref[1024:SLOTS, :], preferred_element_type=f32)
    return position_sums(trig, both[0:PAIR_ROWS] + last, both[PAIR_ROWS:])


def position_kernel(pick_ref, pos_ref, feat_ref, cot_ref, uv_ref, *refs):
    *early_refs, posg_ref, slots_ref = refs
    at = 0
    for early_ref in early_refs:
        at = early_ref.shape[1]
        posg_ref[:, 0:at] = early_ref[...]
    posg_ref[:, at : at + pos_ref.shape[1]] = position_half(pick_ref, pos_ref, feat_ref, cot_ref, uv_ref, slots_ref)


def place_kernel(pick_ref, *refs):
    place = pick_ref[0]
    out_refs, all_refs = refs[8:10], refs[10:12]
    for k, (out_ref, all_ref) in enumerate(zip(out_refs, all_refs)):
        for flip, part_ref in enumerate(refs[4 * k : 4 * k + 4]):
            all_ref[pl.ds(pl.multiple_of(32 * jnp.bitwise_xor(place, flip), 32), 32), :] = part_ref[...]
        rows = out_ref.shape[0]
        width = min(512, rows)
        for at in range(0, rows, width):
            out_ref[at : at + width, :] = all_ref[:, at : at + width].T


def place_rows(pick, first, second):
    shapes = [first[0].shape, second[0].shape]
    whole = lambda shape: pl.BlockSpec(shape, lambda: (0, 0))
    return pl.pallas_call(
        place_kernel,
        in_specs=[pl.BlockSpec(memory_space=pltpu.SMEM)] + [whole(s) for s in shapes for _ in range(4)],
        out_specs=tuple(whole((s[1], 128)) for s in shapes),
        out_shape=tuple(jax.ShapeDtypeStruct((s[1], 128), f32) for s in shapes),
        scratch_shapes=[pltpu.VMEM((128, s[1]), f32) for s in shapes],
        compiler_params=pltpu.CompilerParams(vmem_limit_bytes=20 * MIB),
        cost_estimate=pl.CostEstimate(flops=6 * 10**9, bytes_accessed=4 * 10**6, transcendentals=0),
        name="place_rows",
    )(pick, *first, *second)


def position_sums(trig, u, v):
    _, (c1, s1), (c2, s2) = trig
    orders = lax.broadcasted_iota(jnp.int32, c1.shape, 0).astype(f32) + 1.0
    acc0 = c2 * v[256:264] + s2 * v[264:272] + c1 * v[272:280] + s1 * v[280:288]
    acc1 = orders * (c1 * u[280:288] - s1 * u[272:280])
    acc2 = c2 * u[264:272] - s2 * u[256:264]
    for m in range(8):
        lead_c, lead_s = c1[m : m + 1, :], s1[m : m + 1, :]
        ucc, ucs, usc, uss = [u[64 * k + 8 * m : 64 * k + 8 * m + 8] for k in range(4)]
        vcc, vcs, vsc, vss = [v[64 * k + 8 * m : 64 * k + 8 * m + 8] for k in range(4)]
        acc0 = acc0 + lead_c * (c2 * vcc + s2 * vcs) + lead_s * (c2 * vsc + s2 * vss)
        acc1 = acc1 + float(m + 1) * (lead_c * (c2 * usc + s2 * uss) - lead_s * (c2 * ucc + s2 * ucs))
        acc2 = acc2 + lead_c * (c2 * ucs - s2 * ucc) + lead_s * (c2 * uss - s2 * usc)
    acc2 = acc2 * orders
    rows = [jnp.sum(acc0, 0, keepdims=True) + v[288:289], jnp.sum(acc1, 0, keepdims=True), jnp.sum(acc2, 0, keepdims=True)]
    return phase_step * jnp.concatenate(rows, 0)


def position_rows(pick, positions, features, cotangent, uv, half, early, flops):
    block = positions.shape[1] // 2
    width = block * (1 + len(early))
    return pl.pallas_call(
        position_kernel,
        grid=(1,),
        in_specs=[
            pl.BlockSpec(memory_space=pltpu.SMEM),
            pl.BlockSpec((3, block), lambda i: (0, half)),
            pl.BlockSpec((block, 128), lambda i: (half, 0)),
            pl.BlockSpec((block, 128), lambda i: (half, 0)),
            pl.BlockSpec((2 * PAIR_ROWS, 128 * TILES), lambda i: (0, 0)),
        ]
        + [pl.BlockSpec((3, block), lambda i: (0, 0)) for _ in early],
        out_specs=pl.BlockSpec((3, width), lambda i: (0, 0)),
        out_shape=jax.ShapeDtypeStruct((3, width), f32),
        scratch_shapes=[pltpu.VMEM((SLOTS, block), bf16)],
        compiler_params=pltpu.CompilerParams(vmem_limit_bytes=24 * MIB),
        cost_estimate=pl.CostEstimate(flops=flops, bytes_accessed=block * 700, transcendentals=0),
        name="position_rows",
    )(pick, positions, features, cotangent, uv, *early)


def swap(value, axis):
    return lax.ppermute(value, axis, [(0, 1), (1, 0)])


def swap_both(value):
    return lax.ppermute(value, ("yl", "core"), [(i, 3 - i) for i in range(4)])


def sum_scatter(value, axis):
    n = lax.axis_size(axis)
    parts = lax.all_to_all(value.reshape(n, value.shape[0] // n, 128), axis, 0, 0)
    return jnp.sum(parts, 0)


def gather(value, axis):
    n = lax.axis_size(axis)
    copies = jnp.broadcast_to(value[None], (n,) + value.shape)
    return lax.all_to_all(copies, axis, 0, 0).reshape(n * value.shape[0], 128)


def shards(block, positions, features, cotangent, miller, radial_filter):
    atoms = positions.shape[1]
    block = min(block, atoms)
    waves = miller.shape[1]
    y_at, core_at = lax.axis_index("yl"), lax.axis_index("core")
    atom_count = atoms * lax.axis_size(("z", "yh", "x"))
    wave_count = waves * lax.axis_size(("yl", "core"))
    scale = float(atom_count * wave_count) ** (-0.5)
    pick = (2 * y_at + core_at).astype(jnp.int32).reshape(1)

    turned = radial_filter.T.reshape(2, 64, waves)
    indices = jnp.concatenate([miller.astype(f32), jnp.zeros((5, waves), f32)], 0)
    keep = jnp.where(y_at == 0, turned[0], turned[1])
    send = jnp.where(y_at == 0, turned[1], turned[0])
    here = jnp.concatenate([keep, indices], 0)
    there = swap(jnp.concatenate([send, indices], 0), "yl")
    pair = jnp.concatenate([here, there], 1)
    first, second, pair_indices = pair[:32], pair[32:64], pair[64:]
    keep = jnp.where(core_at == 0, first, second)
    send = jnp.where(core_at == 0, second, first)
    beside = swap(jnp.concatenate([send, pair_indices], 0), "core")
    radial_rows = jnp.concatenate([keep, beside[:32]], 1)
    miller_rows = jnp.concatenate([pair_indices, beside[32:]], 1)
    classes = class_sums(miller_rows, radial_rows, scale, min(1024, 4 * waves))

    part = factors(pick, positions, features, cotangent, block, 1)
    part = sum_scatter(part, ("x", "yh"))
    part = sum_scatter(part, "z")
    part = gather(part, "z")
    total = gather(part, ("x", "yh"))
    grad, uv = feature_rows(positions, total, classes, atoms)
    grad_y, grad_core = swap(grad, "yl"), swap(grad, "core")
    total = lax.optimization_barrier((total, grad))[0]
    own, across, beside, far = filter_rows(miller_rows, total, scale)
    uv = lax.optimization_barrier((uv, own))[0]
    across, beside, far = swap(across, "yl"), swap(beside, "core"), swap_both(far)
    early = position_rows(pick, positions, features, cotangent, uv, 0, [], 10**9)
    grad_y, early = lax.optimization_barrier((grad_y, early))
    grad_far = swap(grad_y, "core")
    posg = position_rows(pick, positions, features, cotangent, uv, 1, [early], 10**9)
    across, far, grad_far, posg = lax.optimization_barrier((across, far, grad_far, posg))
    posg_far, posg_y, posg_core = swap_both(posg), swap(posg, "yl"), swap(posg, "core")
    feature_grad, filter_grad = place_rows(pick, (grad, grad_core, grad_y, grad_far), (own, beside, across, far))
    posg_far, posg_y, posg_core, filter_grad = lax.optimization_barrier((posg_far, posg_y, posg_core, filter_grad))
    position_grad = (posg + posg_core) + (posg_y + posg_far)
    return feature_grad, position_grad, filter_grad


def solution(mesh):
    x, yh = 4, 2
    z = mesh.shape["atom"] // (x * yh)
    fine = Mesh(mesh.devices.reshape(z, yh, x, 2, 2), ("z", "yh", "x", "yl", "core"))
    atom, wave = ("z", "yh", "x"), ("yl", "core")
    placed = (P(None, atom), P(atom, None), P(atom, None), P(None, wave), P(wave, None))
    return jax.shard_map(
        functools.partial(shards, 2048),
        mesh=fine,
        in_specs=placed,
        out_specs=(P(atom, None), P(None, atom), P(wave, None)),
        check_vma=False,
    )
```

```python
import functools
import math

import jax
import jax.numpy as jnp
from jax import lax
from jax.experimental import pallas as pl
from jax.experimental.pallas import tpu as pltpu
from jax.sharding import Mesh, PartitionSpec as P

phase_step = 2.0 * math.pi / 256.0
PAIRS = 296
PAIR_ROWS = 304
TILES = 9
SLOTS = 17 * 64
CLASSES = 896
PACKED = 2560
f32 = jnp.float32
bf16 = jnp.bfloat16
MIB = 1024 * 1024


def nt_dot(a, b):
    return lax.dot_general(a, b, (((1,), (1,)), ((), ())), preferred_element_type=f32)


def turn_trig(turns):
    x = (turns - jnp.floor(turns + 0.5)) * (2.0 * math.pi)
    square = x * x
    cosine = jnp.full_like(x, 1.0 / math.factorial(18) * -1.0)
    for power in range(16, -1, -2):
        cosine = cosine * square + ((-1.0) ** (power // 2) / math.factorial(power))
    sine = jnp.full_like(x, 1.0 / math.factorial(17))
    for power in range(15, 0, -2):
        sine = sine * square + ((-1.0) ** (power // 2) / math.factorial(power))
    return cosine, sine * x


def multiples(position_rows):
    count = position_rows.shape[1]
    orders = lax.broadcasted_iota(jnp.int32, (8, count), 0).astype(f32) + 1.0
    return [turn_trig(orders * (position_rows[d : d + 1, :] * (1.0 / 256.0))) for d in range(3)]


def pair_table(trig1, trig2):
    (c1, s1), (c2, s2) = trig1, trig2
    count = c1.shape[1]
    tiles = []
    for left in (c1, s1):
        for right in (c2, s2):
            for m in range(8):
                tiles.append(left[m : m + 1, :] * right)
    one = (lax.broadcasted_iota(jnp.int32, (16, count), 0) == 0).astype(f32)
    tiles += [c2, s2, c1, s1, one]
    return jnp.concatenate(tiles, 0)


def row_tables(pick_ref, features, cotangent):
    lane = lax.broadcasted_iota(jnp.int32, (32, 128), 1)
    row = lax.broadcasted_iota(jnp.int32, (32, 128), 0)
    pick = (lane == row + 32 * pick_ref[0]).astype(bf16)
    return jnp.concatenate([nt_dot(pick, features), nt_dot(pick, cotangent)], 0)


def fill_slots(slots_ref, trig0, rows):
    c0, s0 = trig0
    for t in range(8):
        slots_ref[128 * t : 128 * t + 64, :] = (c0[t : t + 1, :] * rows).astype(bf16)
        slots_ref[128 * t + 64 : 128 * t + 128, :] = (s0[t : t + 1, :] * rows).astype(bf16)
    slots_ref[1024:1088, :] = rows.astype(bf16)


def factor_kernel(pick_ref, pos_ref, feat_ref, cot_ref, out_ref, total_ref, *slots_refs):
    step = pl.program_id(0)
    size = slots_refs[0].shape[1]
    product = None
    for k, slots_ref in enumerate(slots_refs):
        at = slice(k * size, (k + 1) * size)
        trig = multiples(pos_ref[:, at])
        fill_slots(slots_ref, trig[0], row_tables(pick_ref, feat_ref[at, :], cot_ref[at, :]))
        pairs = pair_table(trig[1], trig[2]).astype(bf16)
        part = nt_dot(pairs, slots_ref[...])
        product = part if product is None else product + part

    @pl.when(step == 0)
    def _():
        total_ref[...] = product

    final = pl.num_programs(0) - 1

    @pl.when(jnp.logical_and(step > 0, step < final))
    def _():
        total_ref[...] += product

    @pl.when(step == final)
    def _():
        for t in range(8):
            at = slice(128 * t, 128 * t + 128)
            out_ref[PAIRS * t : PAIRS * (t + 1), :] = total_ref[0:PAIRS, at] + product[0:PAIRS, at]
        last = total_ref[:, 1024:1088] + product[:, 1024:1088]
        out_ref[2368:2520, :] = jnp.concatenate([last[0:152], last[152:304]], 1)
        out_ref[2520:2560, :] = jnp.zeros((40, 128), f32)


def factors(pick, positions, features, cotangent, block, cuts):
    atoms = positions.shape[1]
    return pl.pallas_call(
        factor_kernel,
        grid=(atoms // block,),
        in_specs=[
            pl.BlockSpec(memory_space=pltpu.SMEM),
            pl.BlockSpec((3, block), lambda i: (0, i)),
            pl.BlockSpec((block, 128), lambda i: (i, 0)),
            pl.BlockSpec((block, 128), lambda i: (i, 0)),
        ],
        out_specs=pl.BlockSpec((PACKED, 128), lambda i: (0, 0)),
        out_shape=jax.ShapeDtypeStruct((PACKED, 128), f32),
        scratch_shapes=[pltpu.VMEM((PAIR_ROWS, SLOTS), f32)] + [pltpu.VMEM((SLOTS, block // cuts), bf16)] * cuts,
        compiler_params=pltpu.CompilerParams(vmem_limit_bytes=56 * MIB),
        cost_estimate=pl.CostEstimate(flops=2 * PAIR_ROWS * SLOTS * atoms, bytes_accessed=atoms * 520, transcendentals=0),
        name="factors",
    )(pick, positions, features, cotangent)


def wave_class(m):
    m0, m1, m2 = [m[d : d + 1, :] for d in range(3)]
    size0, size1, size2 = jnp.abs(m0), jnp.abs(m1), jnp.abs(m2)
    signs = [jnp.clip(v, -1.0, 1.0) for v in (m0, m1, m2)]
    both = (size1 - 1.0) * 8.0 + size2 - 1.0
    inner = jnp.where(
        size1 > 0.0,
        jnp.where(size2 > 0.0, both, 72.0 + size1 - 1.0),
        jnp.where(size2 > 0.0, 64.0 + size2 - 1.0, 80.0),
    )
    tile = jnp.where(size0 > 0.0, size0 - 1.0, 8.0)
    index = (tile * 88.0 + inner).astype(jnp.int32)
    return index, (signs[1] * signs[2], signs[0] * signs[1], signs[0] * signs[2])


def split_hi_lo(v):
    hi = v.astype(bf16)
    return hi, (v - hi.astype(f32)).astype(bf16)


def class_kernel(scale, miller_ref, radial_ref, out_ref, sum_ref):
    step = pl.program_id(0)
    index, products = wave_class(miller_ref[0:3, :])
    radial = radial_ref[...]
    signed = jnp.concatenate([radial] + [radial * p for p in products], 0)
    hi, lo = split_hi_lo(signed)
    hot = (lax.broadcasted_iota(jnp.int32, (CLASSES, index.shape[1]), 0) == index).astype(f32).astype(bf16)
    part = nt_dot(hot, jnp.concatenate([hi, lo], 0))
    part = part[:, :128] + part[:, 128:]

    @pl.when(step == 0)
    def _():
        sum_ref[...] = part

    @pl.when(step > 0)
    def _():
        sum_ref[...] += part

    @pl.when(step == pl.num_programs(0) - 1)
    def _():
        for q in range(4):
            one = sum_ref[:, 32 * q : 32 * q + 32] * scale
            out_ref[q] = jnp.concatenate([one, one, one, one], 1)


def class_sums(miller_rows, radial_rows, scale, block):
    waves = miller_rows.shape[1]
    return pl.pallas_call(
        functools.partial(class_kernel, scale),
        grid=(waves // block,),
        in_specs=[pl.BlockSpec((8, block), lambda i: (0, i)), pl.BlockSpec((32, block), lambda i: (0, i))],
        out_specs=pl.BlockSpec((4, CLASSES, 128), lambda i: (0, 0, 0)),
        out_shape=jax.ShapeDtypeStruct((4, CLASSES, 128), f32),
        scratch_shapes=[pltpu.VMEM((CLASSES, 128), f32)],
        compiler_params=pltpu.CompilerParams(vmem_limit_bytes=18 * MIB),
        cost_estimate=pl.CostEstimate(flops=2 * CLASSES * 256 * waves, bytes_accessed=waves * 160, transcendentals=0),
        name="class_sums",
    )(miller_rows, radial_rows)


def load_tile(total_ref, t):
    if t < 8:
        return total_ref[PAIRS * t : PAIRS * (t + 1), :]
    fold = total_ref[2368:2520, :]
    last = jnp.concatenate([fold[:, :64], fold[0:144, 64:]], 0)
    return jnp.concatenate([last, jnp.zeros((PAIRS, 64), f32)], 1)


def lane_signs():
    lane = lax.broadcasted_iota(jnp.int32, (1, 128), 1)
    return lane, jnp.where(lane < 64, 1.0, -1.0).astype(f32)


def cut(v):
    return [v[0:64], v[64:128], v[128:192], v[192:256]] + [v[256 + 8 * k : 264 + 8 * k] for k in range(5)]


def combine(total_ref, class_ref, uv_ref, down_ref):
    lane, half = lane_signs()
    swap = (lane % 64) < 32
    pick_lane = lax.broadcasted_iota(jnp.int32, (64, 128), 1)
    pick_row = lax.broadcasted_iota(jnp.int32, (64, 128), 0)
    pick = (pick_lane == jnp.where(pick_row < 32, pick_row + 32, pick_row + 64)).astype(bf16)
    for t in range(TILES):
        a = load_tile(total_ref, t)
        x0, x1, x2, x3 = [class_ref[q, 88 * t : 88 * t + 88, :] for q in range(4)]
        i0, i1, i2, i3 = [v[0:64] for v in (x0, x1, x2, x3)]
        cc, cs, sc, ss, e2c, e2s, e1c, e1s, co = cut(a)
        f0, f3 = x0[64:72], x3[64:72]
        g0, g2 = x0[72:80], x2[72:80]
        if t < 8:
            bcc, bcs, bsc, bss, be2c, be2s, be1c, be1s, _ = cut(half * pltpu.roll(a, 64, 1))
            blocks = [
                i0 * cc - i1 * ss - i2 * bsc - i3 * bcs,
                i0 * cs + i1 * sc - i2 * bss + i3 * bcc,
                i0 * sc + i1 * cs + i2 * bcc - i3 * bss,
                i0 * ss - i1 * cc + i2 * bcs + i3 * bsc,
                f0 * e2c - f3 * be2s,
                f0 * e2s + f3 * be2c,
                g0 * e1c - g2 * be1s,
                g0 * e1s + g2 * be1c,
            ]
        else:
            blocks = [i0 * cc - i1 * ss, i0 * cs + i1 * sc, i0 * sc + i1 * cs, i0 * ss - i1 * cc]
            blocks += [f0 * e2c, f0 * e2s, g0 * e1c, g0 * e1s]
        w = jnp.concatenate(blocks + [x0[80:88] * co, jnp.zeros((8, 128), f32)], 0)
        swapped = jnp.where(swap, pltpu.roll(w, 96, 1), pltpu.roll(w, 32, 1))
        uv_ref[0:PAIR_ROWS, 128 * t : 128 * t + 128] = swapped.astype(bf16)
        if t < 8:
            slope = (t + 1.0) * half * pltpu.roll(swapped, 64, 1)
        else:
            slope = jnp.zeros((PAIR_ROWS, 128), f32)
        uv_ref[PAIR_ROWS : 2 * PAIR_ROWS, 128 * t : 128 * t + 128] = slope.astype(bf16)
        down_ref[64 * t : 64 * t + 64, :] = nt_dot(pick, w.astype(bf16)).astype(bf16)


def pair_products(total_ref, pair_ref):
    _, half = lane_signs()
    pair_ref[...] = jnp.zeros((CLASSES, 128), f32)
    for t in range(TILES):
        a = load_tile(total_ref, t)
        b = half * pltpu.roll(a, 64, 1)
        sa = pltpu.roll(a, 32, 1)
        sb = pltpu.roll(b, 32, 1)
        cc, cs, sc, ss, e2c, e2s, e1c, e1s, co = cut(a)
        scc, scs, ssc, sss, se2c, se2s, se1c, se1s, sco = cut(sa)
        tcc, tcs, tsc, tss, te2c, te2s, te1c, te1s, _ = cut(sb)
        zero = jnp.zeros((8, 128), f32)
        y = [
            [cc * scc + cs * scs + sc * ssc + ss * sss, e2c * se2c + e2s * se2s, e1c * se1c + e1s * se1s, co * sco],
            [cs * ssc + sc * scs - cc * sss - ss * scc, zero, zero, zero],
            [sc * tcc + ss * tcs - cc * tsc - cs * tss, zero, e1s * te1c - e1c * te1s, zero],
            [cs * tcc + ss * tsc - cc * tcs - sc * tss, e2s * te2c - e2c * te2s, zero, zero],
        ]
        parts = []
        for q in range(4):
            z = jnp.concatenate(y[q], 0)
            parts.append(z[:, 32:64] + z[:, 96:128])
        pair_ref[88 * t : 88 * t + 88, :] = jnp.concatenate(parts, 1)


def filter_kernel(scale, miller_ref, total_ref, *refs):
    *out_refs, pair_ref, turned_ref = refs
    step = pl.program_id(0)

    @pl.when(step == 0)
    def _():
        pair_products(total_ref, pair_ref)
        turned_ref[...] = pair_ref[...].T.astype(bf16)

    index, products = wave_class(miller_ref[0:3, :])
    hot = (lax.broadcasted_iota(jnp.int32, (CLASSES, index.shape[1]), 0) == index).astype(f32).astype(bf16)
    values = jnp.dot(turned_ref[...], hot, preferred_element_type=f32)
    rows = values[0:32]
    for q in range(3):
        rows = rows + products[q] * values[32 * (q + 1) : 32 * (q + 2)]
    rows = scale * rows

    for k, out_ref in enumerate(out_refs):

        @pl.when(step == k)
        def _():
            out_ref[...] = rows


def filter_rows(miller_rows, total, scale):
    block = miller_rows.shape[1] // 4
    one = jax.ShapeDtypeStruct((32, block), f32)
    return pl.pallas_call(
        functools.partial(filter_kernel, scale),
        grid=(4,),
        in_specs=[pl.BlockSpec((8, block), lambda i: (0, i)), pl.BlockSpec((PACKED, 128), lambda i: (0, 0))],
        out_specs=(pl.BlockSpec((32, block), lambda i: (0, 0)),) * 4,
        out_shape=(one,) * 4,
        scratch_shapes=[pltpu.VMEM((CLASSES, 128), f32), pltpu.VMEM((128, CLASSES), bf16)],
        compiler_params=pltpu.CompilerParams(vmem_limit_bytes=18 * MIB),
        cost_estimate=pl.CostEstimate(flops=2 * CLASSES * 1024 * block, bytes_accessed=block * 640, transcendentals=0),
        name="filter_rows",
    )(miller_rows, total)


def feature_kernel(pos_ref, total_ref, class_ref, grad_ref, uv_ref, down_ref):
    @pl.when(pl.program_id(0) == 0)
    def _():
        combine(total_ref, class_ref, uv_ref, down_ref)

    (c0, s0), trig1, trig2 = multiples(pos_ref[...])
    pairs = pair_table(trig1, trig2).astype(bf16)
    parts = jnp.dot(down_ref[...], pairs, preferred_element_type=f32)
    grad = parts[512:544]
    for t in range(8):
        grad = grad + c0[t : t + 1, :] * parts[64 * t : 64 * t + 32] + s0[t : t + 1, :] * parts[64 * t + 32 : 64 * t + 64]
    grad_ref[...] = grad


def feature_rows(positions, total, classes, block):
    atoms = positions.shape[1]
    return pl.pallas_call(
        feature_kernel,
        grid=(atoms // block,),
        in_specs=[
            pl.BlockSpec((3, block), lambda i: (0, i)),
            pl.BlockSpec((PACKED, 128), lambda i: (0, 0)),
            pl.BlockSpec((4, CLASSES, 128), lambda i: (0, 0, 0)),
        ],
        out_specs=(
            pl.BlockSpec((32, block), lambda i: (0, i)),
            pl.BlockSpec((2 * PAIR_ROWS, 128 * TILES), lambda i: (0, 0)),
        ),
        out_shape=(
            jax.ShapeDtypeStruct((32, atoms), f32),
            jax.ShapeDtypeStruct((2 * PAIR_ROWS, 128 * TILES), bf16),
        ),
        scratch_shapes=[pltpu.VMEM((64 * TILES, PAIR_ROWS), bf16)],
        compiler_params=pltpu.CompilerParams(vmem_limit_bytes=38 * MIB),
        cost_estimate=pl.CostEstimate(flops=2 * PAIR_ROWS * SLOTS * atoms, bytes_accessed=atoms * 700, transcendentals=0),
        name="feature_rows",
    )(positions, total, classes)


def position_kernel(pick_ref, pos_ref, feat_ref, cot_ref, uv_ref, posg_ref, slots_ref):
    trig = multiples(pos_ref[...])
    fill_slots(slots_ref, trig[0], row_tables(pick_ref, feat_ref[...], cot_ref[...]))
    both = jnp.dot(uv_ref[:, 0:1024], slots_ref[0:1024, :], preferred_element_type=f32)
    last = jnp.dot(uv_ref[0:PAIR_ROWS, 1024:SLOTS], slots_ref[1024:SLOTS, :], preferred_element_type=f32)
    posg_ref[...] = position_sums(trig, both[0:PAIR_ROWS] + last, both[PAIR_ROWS:])


def place_kernel(pick_ref, *refs):
    place = pick_ref[0]
    out_refs, all_refs = refs[8:10], refs[10:12]
    for k, (out_ref, all_ref) in enumerate(zip(out_refs, all_refs)):
        for flip, part_ref in enumerate(refs[4 * k : 4 * k + 4]):
            all_ref[pl.ds(pl.multiple_of(32 * jnp.bitwise_xor(place, flip), 32), 32), :] = part_ref[...]
        rows = out_ref.shape[0]
        width = min(512, rows)
        for at in range(0, rows, width):
            out_ref[at : at + width, :] = all_ref[:, at : at + width].T


def place_rows(pick, first, second):
    shapes = [first[0].shape, second[0].shape]
    whole = lambda shape: pl.BlockSpec(shape, lambda: (0, 0))
    return pl.pallas_call(
        place_kernel,
        in_specs=[pl.BlockSpec(memory_space=pltpu.SMEM)] + [whole(s) for s in shapes for _ in range(4)],
        out_specs=tuple(whole((s[1], 128)) for s in shapes),
        out_shape=tuple(jax.ShapeDtypeStruct((s[1], 128), f32) for s in shapes),
        scratch_shapes=[pltpu.VMEM((128, s[1]), f32) for s in shapes],
        compiler_params=pltpu.CompilerParams(vmem_limit_bytes=20 * MIB),
        cost_estimate=pl.CostEstimate(flops=6 * 10**9, bytes_accessed=4 * 10**6, transcendentals=0),
        name="place_rows",
    )(pick, *first, *second)


def position_sums(trig, u, v):
    _, (c1, s1), (c2, s2) = trig
    orders = lax.broadcasted_iota(jnp.int32, c1.shape, 0).astype(f32) + 1.0
    acc0 = c2 * v[256:264] + s2 * v[264:272] + c1 * v[272:280] + s1 * v[280:288]
    acc1 = orders * (c1 * u[280:288] - s1 * u[272:280])
    acc2 = c2 * u[264:272] - s2 * u[256:264]
    for m in range(8):
        lead_c, lead_s = c1[m : m + 1, :], s1[m : m + 1, :]
        ucc, ucs, usc, uss = [u[64 * k + 8 * m : 64 * k + 8 * m + 8] for k in range(4)]
        vcc, vcs, vsc, vss = [v[64 * k + 8 * m : 64 * k + 8 * m + 8] for k in range(4)]
        acc0 = acc0 + lead_c * (c2 * vcc + s2 * vcs) + lead_s * (c2 * vsc + s2 * vss)
        acc1 = acc1 + float(m + 1) * (lead_c * (c2 * usc + s2 * uss) - lead_s * (c2 * ucc + s2 * ucs))
        acc2 = acc2 + lead_c * (c2 * ucs - s2 * ucc) + lead_s * (c2 * uss - s2 * usc)
    acc2 = acc2 * orders
    rows = [jnp.sum(acc0, 0, keepdims=True) + v[288:289], jnp.sum(acc1, 0, keepdims=True), jnp.sum(acc2, 0, keepdims=True)]
    return phase_step * jnp.concatenate(rows, 0)


def position_rows(pick, positions, features, cotangent, uv, block):
    atoms = positions.shape[1]
    return pl.pallas_call(
        position_kernel,
        grid=(atoms // block,),
        in_specs=[
            pl.BlockSpec(memory_space=pltpu.SMEM),
            pl.BlockSpec((3, block), lambda i: (0, i)),
            pl.BlockSpec((block, 128), lambda i: (i, 0)),
            pl.BlockSpec((block, 128), lambda i: (i, 0)),
            pl.BlockSpec((2 * PAIR_ROWS, 128 * TILES), lambda i: (0, 0)),
        ],
        out_specs=pl.BlockSpec((3, block), lambda i: (0, i)),
        out_shape=jax.ShapeDtypeStruct((3, atoms), f32),
        scratch_shapes=[pltpu.VMEM((SLOTS, block), bf16)],
        compiler_params=pltpu.CompilerParams(vmem_limit_bytes=24 * MIB),
        cost_estimate=pl.CostEstimate(flops=4 * PAIR_ROWS * SLOTS * atoms, bytes_accessed=atoms * 700, transcendentals=0),
        name="position_rows",
    )(pick, positions, features, cotangent, uv)


def swap(value, axis):
    return lax.ppermute(value, axis, [(0, 1), (1, 0)])


def swap_both(value):
    return lax.ppermute(value, ("yl", "core"), [(i, 3 - i) for i in range(4)])


def sum_scatter(value, axis):
    n = lax.axis_size(axis)
    parts = lax.all_to_all(value.reshape(n, value.shape[0] // n, 128), axis, 0, 0)
    return jnp.sum(parts, 0)


def gather(value, axis):
    n = lax.axis_size(axis)
    copies = jnp.broadcast_to(value[None], (n,) + value.shape)
    return lax.all_to_all(copies, axis, 0, 0).reshape(n * value.shape[0], 128)


def shards(block, positions, features, cotangent, miller, radial_filter):
    atoms = positions.shape[1]
    block = min(block, atoms)
    waves = miller.shape[1]
    y_at, core_at = lax.axis_index("yl"), lax.axis_index("core")
    atom_count = atoms * lax.axis_size(("z", "yh", "x"))
    wave_count = waves * lax.axis_size(("yl", "core"))
    scale = float(atom_count * wave_count) ** (-0.5)
    pick = (2 * y_at + core_at).astype(jnp.int32).reshape(1)

    turned = radial_filter.T.reshape(2, 64, waves)
    indices = jnp.concatenate([miller.astype(f32), jnp.zeros((5, waves), f32)], 0)
    keep = jnp.where(y_at == 0, turned[0], turned[1])
    send = jnp.where(y_at == 0, turned[1], turned[0])
    here = jnp.concatenate([keep, indices], 0)
    there = swap(jnp.concatenate([send, indices], 0), "yl")
    pair = jnp.concatenate([here, there], 1)
    first, second, pair_indices = pair[:32], pair[32:64], pair[64:]
    keep = jnp.where(core_at == 0, first, second)
    send = jnp.where(core_at == 0, second, first)
    beside = swap(jnp.concatenate([send, pair_indices], 0), "core")
    radial_rows = jnp.concatenate([keep, beside[:32]], 1)
    miller_rows = jnp.concatenate([pair_indices, beside[32:]], 1)
    classes = class_sums(miller_rows, radial_rows, scale, min(1024, 4 * waves))

    part = factors(pick, positions, features, cotangent, min(block, atoms // 2), 1)
    part = sum_scatter(part, ("x", "yh"))
    part = sum_scatter(part, "z")
    part = gather(part, "z")
    total = gather(part, ("x", "yh"))
    grad, uv = feature_rows(positions, total, classes, atoms)
    grad_y, grad_core = swap(grad, "yl"), swap(grad, "core")
    total = lax.optimization_barrier((total, grad))[0]
    own, across, beside, far = filter_rows(miller_rows, total, scale)
    uv = lax.optimization_barrier((uv, own))[0]
    across, beside, far = swap(across, "yl"), swap(beside, "core"), swap_both(far)
    posg = position_rows(pick, positions, features, cotangent, uv, min(block, atoms))
    across, far, grad_y, posg = lax.optimization_barrier((across, far, grad_y, posg))
    grad_far = swap(grad_y, "core")
    posg_far, posg_y, posg_core = swap_both(posg), swap(posg, "yl"), swap(posg, "core")
    feature_grad, filter_grad = place_rows(pick, (grad, grad_core, grad_y, grad_far), (own, beside, across, far))
    posg_far, posg_y, posg_core, filter_grad = lax.optimization_barrier((posg_far, posg_y, posg_core, filter_grad))
    position_grad = (posg + posg_core) + (posg_y + posg_far)
    return feature_grad, position_grad, filter_grad


def solution(mesh):
    x, yh = 4, 2
    z = mesh.shape["atom"] // (x * yh)
    fine = Mesh(mesh.devices.reshape(z, yh, x, 2, 2), ("z", "yh", "x", "yl", "core"))
    atom, wave = ("z", "yh", "x"), ("yl", "core")
    placed = (P(None, atom), P(atom, None), P(atom, None), P(None, wave), P(wave, None))
    return jax.shard_map(
        functools.partial(shards, 2048),
        mesh=fine,
        in_specs=placed,
        out_specs=(P(atom, None), P(None, atom), P(wave, None)),
        check_vma=False,
    )
```

```python
import functools
import math

import jax
import jax.numpy as jnp
from jax import lax
from jax.experimental import pallas as pl
from jax.experimental.pallas import tpu as pltpu
from jax.sharding import Mesh, PartitionSpec as P

phase_step = 2.0 * math.pi / 256.0
PAIRS = 296
PAIR_ROWS = 304
TILES = 9
SLOTS = 17 * 64
CLASSES = 896
PACKED = 2560
f32 = jnp.float32
bf16 = jnp.bfloat16
MIB = 1024 * 1024


def nt_dot(a, b):
    return lax.dot_general(a, b, (((1,), (1,)), ((), ())), preferred_element_type=f32)


def turn_trig(turns):
    x = (turns - jnp.floor(turns + 0.5)) * (2.0 * math.pi)
    square = x * x
    cosine = jnp.full_like(x, 1.0 / math.factorial(18) * -1.0)
    for power in range(16, -1, -2):
        cosine = cosine * square + ((-1.0) ** (power // 2) / math.factorial(power))
    sine = jnp.full_like(x, 1.0 / math.factorial(17))
    for power in range(15, 0, -2):
        sine = sine * square + ((-1.0) ** (power // 2) / math.factorial(power))
    return cosine, sine * x


def multiples(position_rows):
    count = position_rows.shape[1]
    orders = lax.broadcasted_iota(jnp.int32, (8, count), 0).astype(f32) + 1.0
    return [turn_trig(orders * (position_rows[d : d + 1, :] * (1.0 / 256.0))) for d in range(3)]


def pair_table(trig1, trig2):
    (c1, s1), (c2, s2) = trig1, trig2
    count = c1.shape[1]
    tiles = []
    for left in (c1, s1):
        for right in (c2, s2):
            for m in range(8):
                tiles.append(left[m : m + 1, :] * right)
    one = (lax.broadcasted_iota(jnp.int32, (16, count), 0) == 0).astype(f32)
    tiles += [c2, s2, c1, s1, one]
    return jnp.concatenate(tiles, 0)


def row_tables(pick_ref, features, cotangent):
    lane = lax.broadcasted_iota(jnp.int32, (32, 128), 1)
    row = lax.broadcasted_iota(jnp.int32, (32, 128), 0)
    pick = (lane == row + 32 * pick_ref[0]).astype(bf16)
    return jnp.concatenate([nt_dot(pick, features), nt_dot(pick, cotangent)], 0)


def fill_slots(slots_ref, trig0, rows):
    c0, s0 = trig0
    for t in range(8):
        slots_ref[128 * t : 128 * t + 64, :] = (c0[t : t + 1, :] * rows).astype(bf16)
        slots_ref[128 * t + 64 : 128 * t + 128, :] = (s0[t : t + 1, :] * rows).astype(bf16)
    slots_ref[1024:1088, :] = rows.astype(bf16)


def factor_kernel(pick_ref, pos_ref, feat_ref, cot_ref, out_ref, total_ref, *slots_refs):
    step = pl.program_id(0)
    size = slots_refs[0].shape[1]
    product = None
    for k, slots_ref in enumerate(slots_refs):
        at = slice(k * size, (k + 1) * size)
        trig = multiples(pos_ref[:, at])
        fill_slots(slots_ref, trig[0], row_tables(pick_ref, feat_ref[at, :], cot_ref[at, :]))
        pairs = pair_table(trig[1], trig[2]).astype(bf16)
        part = nt_dot(pairs, slots_ref[...])
        product = part if product is None else product + part

    @pl.when(step == 0)
    def _():
        total_ref[...] = product

    final = pl.num_programs(0) - 1

    @pl.when(jnp.logical_and(step > 0, step < final))
    def _():
        total_ref[...] += product

    @pl.when(step == final)
    def _():
        for t in range(8):
            at = slice(128 * t, 128 * t + 128)
            out_ref[PAIRS * t : PAIRS * (t + 1), :] = total_ref[0:PAIRS, at] + product[0:PAIRS, at]
        last = total_ref[:, 1024:1088] + product[:, 1024:1088]
        out_ref[2368:2520, :] = jnp.concatenate([last[0:152], last[152:304]], 1)
        out_ref[2520:2560, :] = jnp.zeros((40, 128), f32)


def factors(pick, positions, features, cotangent, block, cuts):
    atoms = positions.shape[1]
    return pl.pallas_call(
        factor_kernel,
        grid=(atoms // block,),
        in_specs=[
            pl.BlockSpec(memory_space=pltpu.SMEM),
            pl.BlockSpec((3, block), lambda i: (0, i)),
            pl.BlockSpec((block, 128), lambda i: (i, 0)),
            pl.BlockSpec((block, 128), lambda i: (i, 0)),
        ],
        out_specs=pl.BlockSpec((PACKED, 128), lambda i: (0, 0)),
        out_shape=jax.ShapeDtypeStruct((PACKED, 128), f32),
        scratch_shapes=[pltpu.VMEM((PAIR_ROWS, SLOTS), f32)] + [pltpu.VMEM((SLOTS, block // cuts), bf16)] * cuts,
        compiler_params=pltpu.CompilerParams(vmem_limit_bytes=56 * MIB),
        cost_estimate=pl.CostEstimate(flops=2 * PAIR_ROWS * SLOTS * atoms, bytes_accessed=atoms * 520, transcendentals=0),
        name="factors",
    )(pick, positions, features, cotangent)


def wave_class(m):
    m0, m1, m2 = [m[d : d + 1, :] for d in range(3)]
    size0, size1, size2 = jnp.abs(m0), jnp.abs(m1), jnp.abs(m2)
    signs = [jnp.clip(v, -1.0, 1.0) for v in (m0, m1, m2)]
    both = (size1 - 1.0) * 8.0 + size2 - 1.0
    inner = jnp.where(
        size1 > 0.0,
        jnp.where(size2 > 0.0, both, 72.0 + size1 - 1.0),
        jnp.where(size2 > 0.0, 64.0 + size2 - 1.0, 80.0),
    )
    tile = jnp.where(size0 > 0.0, size0 - 1.0, 8.0)
    index = (tile * 88.0 + inner).astype(jnp.int32)
    return index, (signs[1] * signs[2], signs[0] * signs[1], signs[0] * signs[2])


def split_hi_lo(v):
    hi = v.astype(bf16)
    return hi, (v - hi.astype(f32)).astype(bf16)


def class_kernel(scale, miller_ref, radial_ref, out_ref, sum_ref):
    step = pl.program_id(0)
    index, products = wave_class(miller_ref[0:3, :])
    radial = radial_ref[...]
    signed = jnp.concatenate([radial] + [radial * p for p in products], 0)
    hi, lo = split_hi_lo(signed)
    hot = (lax.broadcasted_iota(jnp.int32, (CLASSES, index.shape[1]), 0) == index).astype(f32).astype(bf16)
    part = nt_dot(hot, jnp.concatenate([hi, lo], 0))
    part = part[:, :128] + part[:, 128:]

    @pl.when(step == 0)
    def _():
        sum_ref[...] = part

    @pl.when(step > 0)
    def _():
        sum_ref[...] += part

    @pl.when(step == pl.num_programs(0) - 1)
    def _():
        for q in range(4):
            one = sum_ref[:, 32 * q : 32 * q + 32] * scale
            out_ref[q] = jnp.concatenate([one, one, one, one], 1)


def class_sums(miller_rows, radial_rows, scale, block):
    waves = miller_rows.shape[1]
    return pl.pallas_call(
        functools.partial(class_kernel, scale),
        grid=(waves // block,),
        in_specs=[pl.BlockSpec((8, block), lambda i: (0, i)), pl.BlockSpec((32, block), lambda i: (0, i))],
        out_specs=pl.BlockSpec((4, CLASSES, 128), lambda i: (0, 0, 0)),
        out_shape=jax.ShapeDtypeStruct((4, CLASSES, 128), f32),
        scratch_shapes=[pltpu.VMEM((CLASSES, 128), f32)],
        compiler_params=pltpu.CompilerParams(vmem_limit_bytes=18 * MIB),
        cost_estimate=pl.CostEstimate(flops=2 * CLASSES * 256 * waves, bytes_accessed=waves * 160, transcendentals=0),
        name="class_sums",
    )(miller_rows, radial_rows)


def load_tile(total_ref, t):
    if t < 8:
        return total_ref[PAIRS * t : PAIRS * (t + 1), :]
    fold = total_ref[2368:2520, :]
    last = jnp.concatenate([fold[:, :64], fold[0:144, 64:]], 0)
    return jnp.concatenate([last, jnp.zeros((PAIRS, 64), f32)], 1)


def lane_signs():
    lane = lax.broadcasted_iota(jnp.int32, (1, 128), 1)
    return lane, jnp.where(lane < 64, 1.0, -1.0).astype(f32)


def cut(v):
    return [v[0:64], v[64:128], v[128:192], v[192:256]] + [v[256 + 8 * k : 264 + 8 * k] for k in range(5)]


def combine(total_ref, class_ref, uv_ref, down_ref):
    lane, half = lane_signs()
    swap = (lane % 64) < 32
    pick_lane = lax.broadcasted_iota(jnp.int32, (64, 128), 1)
    pick_row = lax.broadcasted_iota(jnp.int32, (64, 128), 0)
    pick = (pick_lane == jnp.where(pick_row < 32, pick_row + 32, pick_row + 64)).astype(bf16)
    for t in range(TILES):
        a = load_tile(total_ref, t)
        x0, x1, x2, x3 = [class_ref[q, 88 * t : 88 * t + 88, :] for q in range(4)]
        i0, i1, i2, i3 = [v[0:64] for v in (x0, x1, x2, x3)]
        cc, cs, sc, ss, e2c, e2s, e1c, e1s, co = cut(a)
        f0, f3 = x0[64:72], x3[64:72]
        g0, g2 = x0[72:80], x2[72:80]
        if t < 8:
            bcc, bcs, bsc, bss, be2c, be2s, be1c, be1s, _ = cut(half * pltpu.roll(a, 64, 1))
            blocks = [
                i0 * cc - i1 * ss - i2 * bsc - i3 * bcs,
                i0 * cs + i1 * sc - i2 * bss + i3 * bcc,
                i0 * sc + i1 * cs + i2 * bcc - i3 * bss,
                i0 * ss - i1 * cc + i2 * bcs + i3 * bsc,
                f0 * e2c - f3 * be2s,
                f0 * e2s + f3 * be2c,
                g0 * e1c - g2 * be1s,
                g0 * e1s + g2 * be1c,
            ]
        else:
            blocks = [i0 * cc - i1 * ss, i0 * cs + i1 * sc, i0 * sc + i1 * cs, i0 * ss - i1 * cc]
            blocks += [f0 * e2c, f0 * e2s, g0 * e1c, g0 * e1s]
        w = jnp.concatenate(blocks + [x0[80:88] * co, jnp.zeros((8, 128), f32)], 0)
        swapped = jnp.where(swap, pltpu.roll(w, 96, 1), pltpu.roll(w, 32, 1))
        uv_ref[0:PAIR_ROWS, 128 * t : 128 * t + 128] = swapped.astype(bf16)
        if t < 8:
            slope = (t + 1.0) * half * pltpu.roll(swapped, 64, 1)
        else:
            slope = jnp.zeros((PAIR_ROWS, 128), f32)
        uv_ref[PAIR_ROWS : 2 * PAIR_ROWS, 128 * t : 128 * t + 128] = slope.astype(bf16)
        down_ref[64 * t : 64 * t + 64, :] = nt_dot(pick, w.astype(bf16)).astype(bf16)


def pair_products(total_ref, pair_ref):
    _, half = lane_signs()
    pair_ref[:, 88 * TILES :, :] = jnp.zeros((4, CLASSES - 88 * TILES, 128), f32)
    for t in range(TILES):
        a = load_tile(total_ref, t)
        b = half * pltpu.roll(a, 64, 1)
        sa = pltpu.roll(a, 32, 1)
        sb = pltpu.roll(b, 32, 1)
        cc, cs, sc, ss, e2c, e2s, e1c, e1s, co = cut(a)
        scc, scs, ssc, sss, se2c, se2s, se1c, se1s, sco = cut(sa)
        tcc, tcs, tsc, tss, te2c, te2s, te1c, te1s, _ = cut(sb)
        zero = jnp.zeros((8, 128), f32)
        y = [
            [cc * scc + cs * scs + sc * ssc + ss * sss, e2c * se2c + e2s * se2s, e1c * se1c + e1s * se1s, co * sco],
            [cs * ssc + sc * scs - cc * sss - ss * scc, zero, zero, zero],
            [sc * tcc + ss * tcs - cc * tsc - cs * tss, zero, e1s * te1c - e1c * te1s, zero],
            [cs * tcc + ss * tsc - cc * tcs - sc * tss, e2s * te2c - e2c * te2s, zero, zero],
        ]
        for q in range(4):
            pair_ref[q, 88 * t : 88 * t + 88, :] = jnp.concatenate(y[q], 0)


def filter_kernel(scale, miller_ref, total_ref, *refs):
    *out_refs, pair_ref, turned_ref = refs
    step = pl.program_id(0)

    @pl.when(step == 0)
    def _():
        pair_products(total_ref, pair_ref)
        lane = lax.broadcasted_iota(jnp.int32, (32, 128), 1)
        row = lax.broadcasted_iota(jnp.int32, (32, 128), 0)
        pick = jnp.logical_or(lane == row + 32, lane == row + 96).astype(bf16)
        for q in range(4):
            turned_ref[32 * q : 32 * q + 32, :] = nt_dot(pick, pair_ref[q].astype(bf16)).astype(bf16)

    index, products = wave_class(miller_ref[0:3, :])
    hot = (lax.broadcasted_iota(jnp.int32, (CLASSES, index.shape[1]), 0) == index).astype(f32).astype(bf16)
    values = jnp.dot(turned_ref[...], hot, preferred_element_type=f32)
    rows = values[0:32]
    for q in range(3):
        rows = rows + products[q] * values[32 * (q + 1) : 32 * (q + 2)]
    rows = scale * rows

    for k, out_ref in enumerate(out_refs):

        @pl.when(step == k)
        def _():
            out_ref[...] = rows


def filter_rows(miller_rows, total, scale):
    block = miller_rows.shape[1] // 4
    one = jax.ShapeDtypeStruct((32, block), f32)
    return pl.pallas_call(
        functools.partial(filter_kernel, scale),
        grid=(4,),
        in_specs=[pl.BlockSpec((8, block), lambda i: (0, i)), pl.BlockSpec((PACKED, 128), lambda i: (0, 0))],
        out_specs=(pl.BlockSpec((32, block), lambda i: (0, 0)),) * 4,
        out_shape=(one,) * 4,
        scratch_shapes=[pltpu.VMEM((4, CLASSES, 128), f32), pltpu.VMEM((128, CLASSES), bf16)],
        compiler_params=pltpu.CompilerParams(vmem_limit_bytes=18 * MIB),
        cost_estimate=pl.CostEstimate(flops=2 * CLASSES * 1024 * block, bytes_accessed=block * 640, transcendentals=0),
        name="filter_rows",
    )(miller_rows, total)


def feature_kernel(pos_ref, total_ref, class_ref, grad_ref, uv_ref, down_ref):
    @pl.when(pl.program_id(0) == 0)
    def _():
        combine(total_ref, class_ref, uv_ref, down_ref)

    (c0, s0), trig1, trig2 = multiples(pos_ref[...])
    pairs = pair_table(trig1, trig2).astype(bf16)
    parts = jnp.dot(down_ref[...], pairs, preferred_element_type=f32)
    grad = parts[512:544]
    for t in range(8):
        grad = grad + c0[t : t + 1, :] * parts[64 * t : 64 * t + 32] + s0[t : t + 1, :] * parts[64 * t + 32 : 64 * t + 64]
    grad_ref[...] = grad


def feature_rows(positions, total, classes, block):
    atoms = positions.shape[1]
    return pl.pallas_call(
        feature_kernel,
        grid=(atoms // block,),
        in_specs=[
            pl.BlockSpec((3, block), lambda i: (0, i)),
            pl.BlockSpec((PACKED, 128), lambda i: (0, 0)),
            pl.BlockSpec((4, CLASSES, 128), lambda i: (0, 0, 0)),
        ],
        out_specs=(
            pl.BlockSpec((32, block), lambda i: (0, i)),
            pl.BlockSpec((2 * PAIR_ROWS, 128 * TILES), lambda i: (0, 0)),
        ),
        out_shape=(
            jax.ShapeDtypeStruct((32, atoms), f32),
            jax.ShapeDtypeStruct((2 * PAIR_ROWS, 128 * TILES), bf16),
        ),
        scratch_shapes=[pltpu.VMEM((64 * TILES, PAIR_ROWS), bf16)],
        compiler_params=pltpu.CompilerParams(vmem_limit_bytes=38 * MIB),
        cost_estimate=pl.CostEstimate(flops=2 * PAIR_ROWS * SLOTS * atoms, bytes_accessed=atoms * 700, transcendentals=0),
        name="feature_rows",
    )(positions, total, classes)


def position_kernel(pick_ref, pos_ref, feat_ref, cot_ref, uv_ref, posg_ref, slots_ref):
    trig = multiples(pos_ref[...])
    fill_slots(slots_ref, trig[0], row_tables(pick_ref, feat_ref[...], cot_ref[...]))
    both = jnp.dot(uv_ref[:, 0:1024], slots_ref[0:1024, :], preferred_element_type=f32)
    last = jnp.dot(uv_ref[0:PAIR_ROWS, 1024:SLOTS], slots_ref[1024:SLOTS, :], preferred_element_type=f32)
    posg_ref[...] = position_sums(trig, both[0:PAIR_ROWS] + last, both[PAIR_ROWS:])


def place_kernel(pick_ref, *refs):
    place = pick_ref[0]
    out_refs, all_refs = refs[8:10], refs[10:12]
    for k, (out_ref, all_ref) in enumerate(zip(out_refs, all_refs)):
        for flip, part_ref in enumerate(refs[4 * k : 4 * k + 4]):
            all_ref[pl.ds(pl.multiple_of(32 * jnp.bitwise_xor(place, flip), 32), 32), :] = part_ref[...]
        rows = out_ref.shape[0]
        width = min(512, rows)
        for at in range(0, rows, width):
            out_ref[at : at + width, :] = all_ref[:, at : at + width].T


def place_rows(pick, first, second):
    shapes = [first[0].shape, second[0].shape]
    whole = lambda shape: pl.BlockSpec(shape, lambda: (0, 0))
    return pl.pallas_call(
        place_kernel,
        in_specs=[pl.BlockSpec(memory_space=pltpu.SMEM)] + [whole(s) for s in shapes for _ in range(4)],
        out_specs=tuple(whole((s[1], 128)) for s in shapes),
        out_shape=tuple(jax.ShapeDtypeStruct((s[1], 128), f32) for s in shapes),
        scratch_shapes=[pltpu.VMEM((128, s[1]), f32) for s in shapes],
        compiler_params=pltpu.CompilerParams(vmem_limit_bytes=20 * MIB),
        cost_estimate=pl.CostEstimate(flops=6 * 10**9, bytes_accessed=4 * 10**6, transcendentals=0),
        name="place_rows",
    )(pick, *first, *second)


def position_sums(trig, u, v):
    _, (c1, s1), (c2, s2) = trig
    orders = lax.broadcasted_iota(jnp.int32, c1.shape, 0).astype(f32) + 1.0
    acc0 = c2 * v[256:264] + s2 * v[264:272] + c1 * v[272:280] + s1 * v[280:288]
    acc1 = orders * (c1 * u[280:288] - s1 * u[272:280])
    acc2 = c2 * u[264:272] - s2 * u[256:264]
    for m in range(8):
        lead_c, lead_s = c1[m : m + 1, :], s1[m : m + 1, :]
        ucc, ucs, usc, uss = [u[64 * k + 8 * m : 64 * k + 8 * m + 8] for k in range(4)]
        vcc, vcs, vsc, vss = [v[64 * k + 8 * m : 64 * k + 8 * m + 8] for k in range(4)]
        acc0 = acc0 + lead_c * (c2 * vcc + s2 * vcs) + lead_s * (c2 * vsc + s2 * vss)
        acc1 = acc1 + float(m + 1) * (lead_c * (c2 * usc + s2 * uss) - lead_s * (c2 * ucc + s2 * ucs))
        acc2 = acc2 + lead_c * (c2 * ucs - s2 * ucc) + lead_s * (c2 * uss - s2 * usc)
    acc2 = acc2 * orders
    rows = [jnp.sum(acc0, 0, keepdims=True) + v[288:289], jnp.sum(acc1, 0, keepdims=True), jnp.sum(acc2, 0, keepdims=True)]
    return phase_step * jnp.concatenate(rows, 0)


def position_rows(pick, positions, features, cotangent, uv, block):
    atoms = positions.shape[1]
    return pl.pallas_call(
        position_kernel,
        grid=(atoms // block,),
        in_specs=[
            pl.BlockSpec(memory_space=pltpu.SMEM),
            pl.BlockSpec((3, block), lambda i: (0, i)),
            pl.BlockSpec((block, 128), lambda i: (i, 0)),
            pl.BlockSpec((block, 128), lambda i: (i, 0)),
            pl.BlockSpec((2 * PAIR_ROWS, 128 * TILES), lambda i: (0, 0)),
        ],
        out_specs=pl.BlockSpec((3, block), lambda i: (0, i)),
        out_shape=jax.ShapeDtypeStruct((3, atoms), f32),
        scratch_shapes=[pltpu.VMEM((SLOTS, block), bf16)],
        compiler_params=pltpu.CompilerParams(vmem_limit_bytes=24 * MIB),
        cost_estimate=pl.CostEstimate(flops=4 * PAIR_ROWS * SLOTS * atoms, bytes_accessed=atoms * 700, transcendentals=0),
        name="position_rows",
    )(pick, positions, features, cotangent, uv)


def swap(value, axis):
    return lax.ppermute(value, axis, [(0, 1), (1, 0)])


def swap_both(value):
    return lax.ppermute(value, ("yl", "core"), [(i, 3 - i) for i in range(4)])


def sum_scatter(value, axis):
    n = lax.axis_size(axis)
    parts = lax.all_to_all(value.reshape(n, value.shape[0] // n, 128), axis, 0, 0)
    return jnp.sum(parts, 0)


def gather(value, axis):
    n = lax.axis_size(axis)
    copies = jnp.broadcast_to(value[None], (n,) + value.shape)
    return lax.all_to_all(copies, axis, 0, 0).reshape(n * value.shape[0], 128)


def shards(block, positions, features, cotangent, miller, radial_filter):
    atoms = positions.shape[1]
    block = min(block, atoms)
    waves = miller.shape[1]
    y_at, core_at = lax.axis_index("yl"), lax.axis_index("core")
    atom_count = atoms * lax.axis_size(("z", "yh", "x"))
    wave_count = waves * lax.axis_size(("yl", "core"))
    scale = float(atom_count * wave_count) ** (-0.5)
    pick = (2 * y_at + core_at).astype(jnp.int32).reshape(1)

    turned = radial_filter.T.reshape(2, 64, waves)
    indices = jnp.concatenate([miller.astype(f32), jnp.zeros((5, waves), f32)], 0)
    keep = jnp.where(y_at == 0, turned[0], turned[1])
    send = jnp.where(y_at == 0, turned[1], turned[0])
    here = jnp.concatenate([keep, indices], 0)
    there = swap(jnp.concatenate([send, indices], 0), "yl")
    pair = jnp.concatenate([here, there], 1)
    first, second, pair_indices = pair[:32], pair[32:64], pair[64:]
    keep = jnp.where(core_at == 0, first, second)
    send = jnp.where(core_at == 0, second, first)
    beside = swap(jnp.concatenate([send, pair_indices], 0), "core")
    radial_rows = jnp.concatenate([keep, beside[:32]], 1)
    miller_rows = jnp.concatenate([pair_indices, beside[32:]], 1)
    classes = class_sums(miller_rows, radial_rows, scale, min(1024, 4 * waves))

    part = factors(pick, positions, features, cotangent, min(block, atoms // 2), 1)
    part = sum_scatter(part, ("x", "yh"))
    part = sum_scatter(part, "z")
    part = gather(part, "z")
    total = gather(part, ("x", "yh"))
    grad, uv = feature_rows(positions, total, classes, atoms)
    grad_y, grad_core = swap(grad, "yl"), swap(grad, "core")
    total = lax.optimization_barrier((total, grad))[0]
    own, across, beside, far = filter_rows(miller_rows, total, scale)
    uv = lax.optimization_barrier((uv, own))[0]
    across, beside, far = swap(across, "yl"), swap(beside, "core"), swap_both(far)
    posg = position_rows(pick, positions, features, cotangent, uv, min(block, atoms))
    across, far, grad_y, posg = lax.optimization_barrier((across, far, grad_y, posg))
    grad_far = swap(grad_y, "core")
    posg_far, posg_y, posg_core = swap_both(posg), swap(posg, "yl"), swap(posg, "core")
    feature_grad, filter_grad = place_rows(pick, (grad, grad_core, grad_y, grad_far), (own, beside, across, far))
    posg_far, posg_y, posg_core, filter_grad = lax.optimization_barrier((posg_far, posg_y, posg_core, filter_grad))
    position_grad = (posg + posg_core) + (posg_y + posg_far)
    return feature_grad, position_grad, filter_grad


def solution(mesh):
    x, yh = 4, 2
    z = mesh.shape["atom"] // (x * yh)
    fine = Mesh(mesh.devices.reshape(z, yh, x, 2, 2), ("z", "yh", "x", "yl", "core"))
    atom, wave = ("z", "yh", "x"), ("yl", "core")
    placed = (P(None, atom), P(atom, None), P(atom, None), P(None, wave), P(wave, None))
    return jax.shard_map(
        functools.partial(shards, 2048),
        mesh=fine,
        in_specs=placed,
        out_specs=(P(atom, None), P(None, atom), P(wave, None)),
        check_vma=False,
    )
```

```python
import functools
import math

import jax
import jax.numpy as jnp
from jax import lax
from jax.experimental import pallas as pl
from jax.experimental.pallas import tpu as pltpu
from jax.sharding import Mesh, PartitionSpec as P

phase_step = 2.0 * math.pi / 256.0
PAIRS = 296
PAIR_ROWS = 304
TILES = 9
SLOTS = 17 * 64
CLASSES = 896
PACKED = 2560
f32 = jnp.float32
bf16 = jnp.bfloat16
MIB = 1024 * 1024


def nt_dot(a, b):
    return lax.dot_general(a, b, (((1,), (1,)), ((), ())), preferred_element_type=f32)


def turn_trig(turns):
    x = (turns - jnp.floor(turns + 0.5)) * (2.0 * math.pi)
    square = x * x
    cosine = jnp.full_like(x, 1.0 / math.factorial(18) * -1.0)
    for power in range(16, -1, -2):
        cosine = cosine * square + ((-1.0) ** (power // 2) / math.factorial(power))
    sine = jnp.full_like(x, 1.0 / math.factorial(17))
    for power in range(15, 0, -2):
        sine = sine * square + ((-1.0) ** (power // 2) / math.factorial(power))
    return cosine, sine * x


def multiples(position_rows):
    count = position_rows.shape[1]
    orders = lax.broadcasted_iota(jnp.int32, (8, count), 0).astype(f32) + 1.0
    return [turn_trig(orders * (position_rows[d : d + 1, :] * (1.0 / 256.0))) for d in range(3)]


def pair_table(trig1, trig2):
    (c1, s1), (c2, s2) = trig1, trig2
    count = c1.shape[1]
    tiles = []
    for left in (c1, s1):
        for right in (c2, s2):
            for m in range(8):
                tiles.append(left[m : m + 1, :] * right)
    one = (lax.broadcasted_iota(jnp.int32, (16, count), 0) == 0).astype(f32)
    tiles += [c2, s2, c1, s1, one]
    return jnp.concatenate(tiles, 0)


def row_tables(pick_ref, features, cotangent):
    lane = lax.broadcasted_iota(jnp.int32, (32, 128), 1)
    row = lax.broadcasted_iota(jnp.int32, (32, 128), 0)
    pick = (lane == row + 32 * pick_ref[0]).astype(bf16)
    return jnp.concatenate([nt_dot(pick, features), nt_dot(pick, cotangent)], 0)


def fill_slots(slots_ref, trig0, rows):
    c0, s0 = trig0
    for t in range(8):
        slots_ref[128 * t : 128 * t + 64, :] = (c0[t : t + 1, :] * rows).astype(bf16)
        slots_ref[128 * t + 64 : 128 * t + 128, :] = (s0[t : t + 1, :] * rows).astype(bf16)
    slots_ref[1024:1088, :] = rows.astype(bf16)


def factor_kernel(pick_ref, pos_ref, feat_ref, cot_ref, out_ref, total_ref, *slots_refs):
    step = pl.program_id(0)
    size = slots_refs[0].shape[1]
    product = None
    for k, slots_ref in enumerate(slots_refs):
        at = slice(k * size, (k + 1) * size)
        trig = multiples(pos_ref[:, at])
        fill_slots(slots_ref, trig[0], row_tables(pick_ref, feat_ref[at, :], cot_ref[at, :]))
        pairs = pair_table(trig[1], trig[2]).astype(bf16)
        part = nt_dot(pairs, slots_ref[...])
        product = part if product is None else product + part

    @pl.when(step == 0)
    def _():
        total_ref[...] = product

    final = pl.num_programs(0) - 1

    @pl.when(jnp.logical_and(step > 0, step < final))
    def _():
        total_ref[...] += product

    @pl.when(step == final)
    def _():
        for t in range(8):
            at = slice(128 * t, 128 * t + 128)
            out_ref[PAIRS * t : PAIRS * (t + 1), :] = total_ref[0:PAIRS, at] + product[0:PAIRS, at]
        last = total_ref[:, 1024:1088] + product[:, 1024:1088]
        out_ref[2368:2520, :] = jnp.concatenate([last[0:152], last[152:304]], 1)
        out_ref[2520:2560, :] = jnp.zeros((40, 128), f32)


def factors(pick, positions, features, cotangent, block, cuts):
    atoms = positions.shape[1]
    return pl.pallas_call(
        factor_kernel,
        grid=(atoms // block,),
        in_specs=[
            pl.BlockSpec(memory_space=pltpu.SMEM),
            pl.BlockSpec((3, block), lambda i: (0, i)),
            pl.BlockSpec((block, 128), lambda i: (i, 0)),
            pl.BlockSpec((block, 128), lambda i: (i, 0)),
        ],
        out_specs=pl.BlockSpec((PACKED, 128), lambda i: (0, 0)),
        out_shape=jax.ShapeDtypeStruct((PACKED, 128), f32),
        scratch_shapes=[pltpu.VMEM((PAIR_ROWS, SLOTS), f32)] + [pltpu.VMEM((SLOTS, block // cuts), bf16)] * cuts,
        compiler_params=pltpu.CompilerParams(vmem_limit_bytes=56 * MIB),
        cost_estimate=pl.CostEstimate(flops=2 * PAIR_ROWS * SLOTS * atoms, bytes_accessed=atoms * 520, transcendentals=0),
        name="factors",
    )(pick, positions, features, cotangent)


def wave_class(m):
    m0, m1, m2 = [m[d : d + 1, :] for d in range(3)]
    size0, size1, size2 = jnp.abs(m0), jnp.abs(m1), jnp.abs(m2)
    signs = [jnp.clip(v, -1.0, 1.0) for v in (m0, m1, m2)]
    both = (size1 - 1.0) * 8.0 + size2 - 1.0
    inner = jnp.where(
        size1 > 0.0,
        jnp.where(size2 > 0.0, both, 72.0 + size1 - 1.0),
        jnp.where(size2 > 0.0, 64.0 + size2 - 1.0, 80.0),
    )
    tile = jnp.where(size0 > 0.0, size0 - 1.0, 8.0)
    index = (tile * 88.0 + inner).astype(jnp.int32)
    return index, (signs[1] * signs[2], signs[0] * signs[1], signs[0] * signs[2])


def split_hi_lo(v):
    hi = v.astype(bf16)
    return hi, (v - hi.astype(f32)).astype(bf16)


def class_kernel(scale, miller_ref, radial_ref, out_ref, sum_ref):
    step = pl.program_id(0)
    index, products = wave_class(miller_ref[0:3, :])
    radial = radial_ref[...]
    signed = jnp.concatenate([radial] + [radial * p for p in products], 0)
    hi, lo = split_hi_lo(signed)
    hot = (lax.broadcasted_iota(jnp.int32, (CLASSES, index.shape[1]), 0) == index).astype(f32).astype(bf16)
    part = nt_dot(hot, jnp.concatenate([hi, lo], 0))
    part = part[:, :128] + part[:, 128:]

    @pl.when(step == 0)
    def _():
        sum_ref[...] = part

    @pl.when(step > 0)
    def _():
        sum_ref[...] += part

    @pl.when(step == pl.num_programs(0) - 1)
    def _():
        for q in range(4):
            one = sum_ref[:, 32 * q : 32 * q + 32] * scale
            out_ref[q] = jnp.concatenate([one, one, one, one], 1)


def class_sums(miller_rows, radial_rows, scale, block):
    waves = miller_rows.shape[1]
    return pl.pallas_call(
        functools.partial(class_kernel, scale),
        grid=(waves // block,),
        in_specs=[pl.BlockSpec((8, block), lambda i: (0, i)), pl.BlockSpec((32, block), lambda i: (0, i))],
        out_specs=pl.BlockSpec((4, CLASSES, 128), lambda i: (0, 0, 0)),
        out_shape=jax.ShapeDtypeStruct((4, CLASSES, 128), f32),
        scratch_shapes=[pltpu.VMEM((CLASSES, 128), f32)],
        compiler_params=pltpu.CompilerParams(vmem_limit_bytes=18 * MIB),
        cost_estimate=pl.CostEstimate(flops=2 * CLASSES * 256 * waves, bytes_accessed=waves * 160, transcendentals=0),
        name="class_sums",
    )(miller_rows, radial_rows)


def load_tile(total_ref, t):
    if t < 8:
        return total_ref[PAIRS * t : PAIRS * (t + 1), :]
    fold = total_ref[2368:2520, :]
    last = jnp.concatenate([fold[:, :64], fold[0:144, 64:]], 0)
    return jnp.concatenate([last, jnp.zeros((PAIRS, 64), f32)], 1)


def lane_signs():
    lane = lax.broadcasted_iota(jnp.int32, (1, 128), 1)
    return lane, jnp.where(lane < 64, 1.0, -1.0).astype(f32)


def cut(v):
    return [v[0:64], v[64:128], v[128:192], v[192:256]] + [v[256 + 8 * k : 264 + 8 * k] for k in range(5)]


def combine(total_ref, class_ref, uv_ref, down_ref):
    lane, half = lane_signs()
    swap = (lane % 64) < 32
    pick_lane = lax.broadcasted_iota(jnp.int32, (64, 128), 1)
    pick_row = lax.broadcasted_iota(jnp.int32, (64, 128), 0)
    pick = (pick_lane == jnp.where(pick_row < 32, pick_row + 32, pick_row + 64)).astype(bf16)
    for t in range(TILES):
        a = load_tile(total_ref, t)
        x0, x1, x2, x3 = [class_ref[q, 88 * t : 88 * t + 88, :] for q in range(4)]
        i0, i1, i2, i3 = [v[0:64] for v in (x0, x1, x2, x3)]
        cc, cs, sc, ss, e2c, e2s, e1c, e1s, co = cut(a)
        f0, f3 = x0[64:72], x3[64:72]
        g0, g2 = x0[72:80], x2[72:80]
        if t < 8:
            bcc, bcs, bsc, bss, be2c, be2s, be1c, be1s, _ = cut(half * pltpu.roll(a, 64, 1))
            blocks = [
                i0 * cc - i1 * ss - i2 * bsc - i3 * bcs,
                i0 * cs + i1 * sc - i2 * bss + i3 * bcc,
                i0 * sc + i1 * cs + i2 * bcc - i3 * bss,
                i0 * ss - i1 * cc + i2 * bcs + i3 * bsc,
                f0 * e2c - f3 * be2s,
                f0 * e2s + f3 * be2c,
                g0 * e1c - g2 * be1s,
                g0 * e1s + g2 * be1c,
            ]
        else:
            blocks = [i0 * cc - i1 * ss, i0 * cs + i1 * sc, i0 * sc + i1 * cs, i0 * ss - i1 * cc]
            blocks += [f0 * e2c, f0 * e2s, g0 * e1c, g0 * e1s]
        w = jnp.concatenate(blocks + [x0[80:88] * co, jnp.zeros((8, 128), f32)], 0)
        swapped = jnp.where(swap, pltpu.roll(w, 96, 1), pltpu.roll(w, 32, 1))
        uv_ref[0:PAIR_ROWS, 128 * t : 128 * t + 128] = swapped.astype(bf16)
        if t < 8:
            slope = (t + 1.0) * half * pltpu.roll(swapped, 64, 1)
        else:
            slope = jnp.zeros((PAIR_ROWS, 128), f32)
        uv_ref[PAIR_ROWS : 2 * PAIR_ROWS, 128 * t : 128 * t + 128] = slope.astype(bf16)
        down_ref[64 * t : 64 * t + 64, :] = nt_dot(pick, w.astype(bf16)).astype(bf16)


def pair_products(total_ref, pair_ref):
    _, half = lane_signs()
    pair_ref[:, 88 * TILES :, :] = jnp.zeros((4, CLASSES - 88 * TILES, 128), f32)
    for t in range(TILES):
        a = load_tile(total_ref, t)
        b = half * pltpu.roll(a, 64, 1)
        sa = pltpu.roll(a, 32, 1)
        sb = pltpu.roll(b, 32, 1)
        cc, cs, sc, ss, e2c, e2s, e1c, e1s, co = cut(a)
        scc, scs, ssc, sss, se2c, se2s, se1c, se1s, sco = cut(sa)
        tcc, tcs, tsc, tss, te2c, te2s, te1c, te1s, _ = cut(sb)
        zero = jnp.zeros((8, 128), f32)
        y = [
            [cc * scc + cs * scs + sc * ssc + ss * sss, e2c * se2c + e2s * se2s, e1c * se1c + e1s * se1s, co * sco],
            [cs * ssc + sc * scs - cc * sss - ss * scc, zero, zero, zero],
            [sc * tcc + ss * tcs - cc * tsc - cs * tss, zero, e1s * te1c - e1c * te1s, zero],
            [cs * tcc + ss * tsc - cc * tcs - sc * tss, e2s * te2c - e2c * te2s, zero, zero],
        ]
        for q in range(4):
            pair_ref[q, 88 * t : 88 * t + 88, :] = jnp.concatenate(y[q], 0)


def filter_kernel(scale, miller_ref, total_ref, *refs):
    *out_refs, pair_ref, turned_ref = refs
    step = pl.program_id(0)

    @pl.when(step == 0)
    def _():
        pair_products(total_ref, pair_ref)
        lane = lax.broadcasted_iota(jnp.int32, (32, 128), 1)
        row = lax.broadcasted_iota(jnp.int32, (32, 128), 0)
        pick = jnp.logical_or(lane == row + 32, lane == row + 96).astype(bf16)
        for q in range(4):
            turned_ref[32 * q : 32 * q + 32, :] = nt_dot(pick, pair_ref[q].astype(bf16)).astype(bf16)

    index, products = wave_class(miller_ref[0:3, :])
    hot = (lax.broadcasted_iota(jnp.int32, (CLASSES, index.shape[1]), 0) == index).astype(f32).astype(bf16)
    values = jnp.dot(turned_ref[...], hot, preferred_element_type=f32)
    rows = values[0:32]
    for q in range(3):
        rows = rows + products[q] * values[32 * (q + 1) : 32 * (q + 2)]
    rows = scale * rows

    for k, out_ref in enumerate(out_refs):

        @pl.when(step == k)
        def _():
            out_ref[...] = rows


def filter_rows(miller_rows, total, scale):
    block = miller_rows.shape[1] // 4
    one = jax.ShapeDtypeStruct((32, block), f32)
    return pl.pallas_call(
        functools.partial(filter_kernel, scale),
        grid=(4,),
        in_specs=[pl.BlockSpec((8, block), lambda i: (0, i)), pl.BlockSpec((PACKED, 128), lambda i: (0, 0))],
        out_specs=(pl.BlockSpec((32, block), lambda i: (0, 0)),) * 4,
        out_shape=(one,) * 4,
        scratch_shapes=[pltpu.VMEM((4, CLASSES, 128), f32), pltpu.VMEM((128, CLASSES), bf16)],
        compiler_params=pltpu.CompilerParams(vmem_limit_bytes=18 * MIB),
        cost_estimate=pl.CostEstimate(flops=2 * CLASSES * 1024 * block, bytes_accessed=block * 640, transcendentals=0),
        name="filter_rows",
    )(miller_rows, total)


def feature_kernel(pos_ref, total_ref, class_ref, grad_ref, uv_ref, down_ref):
    @pl.when(pl.program_id(0) == 0)
    def _():
        combine(total_ref, class_ref, uv_ref, down_ref)

    (c0, s0), trig1, trig2 = multiples(pos_ref[...])
    pairs = pair_table(trig1, trig2).astype(bf16)
    parts = jnp.dot(down_ref[...], pairs, preferred_element_type=f32)
    grad = parts[512:544]
    for t in range(8):
        grad = grad + c0[t : t + 1, :] * parts[64 * t : 64 * t + 32] + s0[t : t + 1, :] * parts[64 * t + 32 : 64 * t + 64]
    grad_ref[...] = grad


def feature_rows(positions, total, classes, block):
    atoms = positions.shape[1]
    return pl.pallas_call(
        feature_kernel,
        grid=(atoms // block,),
        in_specs=[
            pl.BlockSpec((3, block), lambda i: (0, i)),
            pl.BlockSpec((PACKED, 128), lambda i: (0, 0)),
            pl.BlockSpec((4, CLASSES, 128), lambda i: (0, 0, 0)),
        ],
        out_specs=(
            pl.BlockSpec((32, block), lambda i: (0, i)),
            pl.BlockSpec((2 * PAIR_ROWS, 128 * TILES), lambda i: (0, 0)),
        ),
        out_shape=(
            jax.ShapeDtypeStruct((32, atoms), f32),
            jax.ShapeDtypeStruct((2 * PAIR_ROWS, 128 * TILES), bf16),
        ),
        scratch_shapes=[pltpu.VMEM((64 * TILES, PAIR_ROWS), bf16)],
        compiler_params=pltpu.CompilerParams(vmem_limit_bytes=38 * MIB),
        cost_estimate=pl.CostEstimate(flops=2 * PAIR_ROWS * SLOTS * atoms, bytes_accessed=atoms * 700, transcendentals=0),
        name="feature_rows",
    )(positions, total, classes)


def position_kernel(pick_ref, pos_ref, feat_ref, cot_ref, uv_ref, posg_ref, slots_ref):
    trig = multiples(pos_ref[...])
    fill_slots(slots_ref, trig[0], row_tables(pick_ref, feat_ref[...], cot_ref[...]))
    both = jnp.dot(uv_ref[:, 0:1024], slots_ref[0:1024, :], preferred_element_type=f32)
    last = jnp.dot(uv_ref[0:PAIR_ROWS, 1024:SLOTS], slots_ref[1024:SLOTS, :], preferred_element_type=f32)
    posg_ref[...] = position_sums(trig, both[0:PAIR_ROWS] + last, both[PAIR_ROWS:])


def place_kernel(pick_ref, *refs):
    place = pick_ref[0]
    out_refs, all_refs = refs[8:10], refs[10:12]
    for k, (out_ref, all_ref) in enumerate(zip(out_refs, all_refs)):
        for flip, part_ref in enumerate(refs[4 * k : 4 * k + 4]):
            all_ref[pl.ds(pl.multiple_of(32 * jnp.bitwise_xor(place, flip), 32), 32), :] = part_ref[...]
        rows = out_ref.shape[0]
        width = min(512, rows)
        for at in range(0, rows, width):
            out_ref[at : at + width, :] = all_ref[:, at : at + width].T


def place_rows(pick, first, second):
    shapes = [first[0].shape, second[0].shape]
    whole = lambda shape: pl.BlockSpec(shape, lambda: (0, 0))
    return pl.pallas_call(
        place_kernel,
        in_specs=[pl.BlockSpec(memory_space=pltpu.SMEM)] + [whole(s) for s in shapes for _ in range(4)],
        out_specs=tuple(whole((s[1], 128)) for s in shapes),
        out_shape=tuple(jax.ShapeDtypeStruct((s[1], 128), f32) for s in shapes),
        scratch_shapes=[pltpu.VMEM((128, s[1]), f32) for s in shapes],
        compiler_params=pltpu.CompilerParams(vmem_limit_bytes=20 * MIB),
        cost_estimate=pl.CostEstimate(flops=6 * 10**9, bytes_accessed=4 * 10**6, transcendentals=0),
        name="place_rows",
    )(pick, *first, *second)


def position_sums(trig, u, v):
    _, (c1, s1), (c2, s2) = trig
    orders = lax.broadcasted_iota(jnp.int32, c1.shape, 0).astype(f32) + 1.0
    acc0 = c2 * v[256:264] + s2 * v[264:272] + c1 * v[272:280] + s1 * v[280:288]
    acc1 = orders * (c1 * u[280:288] - s1 * u[272:280])
    acc2 = c2 * u[264:272] - s2 * u[256:264]
    for m in range(8):
        lead_c, lead_s = c1[m : m + 1, :], s1[m : m + 1, :]
        ucc, ucs, usc, uss = [u[64 * k + 8 * m : 64 * k + 8 * m + 8] for k in range(4)]
        vcc, vcs, vsc, vss = [v[64 * k + 8 * m : 64 * k + 8 * m + 8] for k in range(4)]
        acc0 = acc0 + lead_c * (c2 * vcc + s2 * vcs) + lead_s * (c2 * vsc + s2 * vss)
        acc1 = acc1 + float(m + 1) * (lead_c * (c2 * usc + s2 * uss) - lead_s * (c2 * ucc + s2 * ucs))
        acc2 = acc2 + lead_c * (c2 * ucs - s2 * ucc) + lead_s * (c2 * uss - s2 * usc)
    acc2 = acc2 * orders
    rows = [jnp.sum(acc0, 0, keepdims=True) + v[288:289], jnp.sum(acc1, 0, keepdims=True), jnp.sum(acc2, 0, keepdims=True)]
    return phase_step * jnp.concatenate(rows, 0)


def position_rows(pick, positions, features, cotangent, uv, block):
    atoms = positions.shape[1]
    return pl.pallas_call(
        position_kernel,
        grid=(atoms // block,),
        in_specs=[
            pl.BlockSpec(memory_space=pltpu.SMEM),
            pl.BlockSpec((3, block), lambda i: (0, i)),
            pl.BlockSpec((block, 128), lambda i: (i, 0)),
            pl.BlockSpec((block, 128), lambda i: (i, 0)),
            pl.BlockSpec((2 * PAIR_ROWS, 128 * TILES), lambda i: (0, 0)),
        ],
        out_specs=pl.BlockSpec((3, block), lambda i: (0, i)),
        out_shape=jax.ShapeDtypeStruct((3, atoms), f32),
        scratch_shapes=[pltpu.VMEM((SLOTS, block), bf16)],
        compiler_params=pltpu.CompilerParams(vmem_limit_bytes=24 * MIB),
        cost_estimate=pl.CostEstimate(flops=4 * PAIR_ROWS * SLOTS * atoms, bytes_accessed=atoms * 700, transcendentals=0),
        name="position_rows",
    )(pick, positions, features, cotangent, uv)


def swap(value, axis):
    return lax.ppermute(value, axis, [(0, 1), (1, 0)])


def swap_both(value):
    return lax.ppermute(value, ("yl", "core"), [(i, 3 - i) for i in range(4)])


def sum_scatter(value, axis):
    n = lax.axis_size(axis)
    parts = lax.all_to_all(value.reshape(n, value.shape[0] // n, 128), axis, 0, 0)
    return jnp.sum(parts, 0)


def total_kernel(parts_ref, out_ref):
    total = jnp.sum(parts_ref[...], 0)
    for k in range(out_ref.shape[0]):
        out_ref[k] = total


def sum_everywhere(value, axis):
    n = lax.axis_size(axis)
    parts = lax.all_to_all(value.reshape(n, value.shape[0] // n, 128), axis, 0, 0)
    copies = pl.pallas_call(
        total_kernel,
        out_shape=jax.ShapeDtypeStruct(parts.shape, f32),
        compiler_params=pltpu.CompilerParams(vmem_limit_bytes=4 * MIB),
        name="total_rows",
    )(parts)
    return lax.all_to_all(copies, axis, 0, 0).reshape(value.shape)


def gather(value, axis):
    n = lax.axis_size(axis)
    copies = jnp.broadcast_to(value[None], (n,) + value.shape)
    return lax.all_to_all(copies, axis, 0, 0).reshape(n * value.shape[0], 128)


def shards(block, positions, features, cotangent, miller, radial_filter):
    atoms = positions.shape[1]
    block = min(block, atoms)
    waves = miller.shape[1]
    y_at, core_at = lax.axis_index("yl"), lax.axis_index("core")
    atom_count = atoms * lax.axis_size(("z", "yh", "x"))
    wave_count = waves * lax.axis_size(("yl", "core"))
    scale = float(atom_count * wave_count) ** (-0.5)
    pick = (2 * y_at + core_at).astype(jnp.int32).reshape(1)

    turned = radial_filter.T.reshape(2, 64, waves)
    indices = jnp.concatenate([miller.astype(f32), jnp.zeros((5, waves), f32)], 0)
    keep = jnp.where(y_at == 0, turned[0], turned[1])
    send = jnp.where(y_at == 0, turned[1], turned[0])
    here = jnp.concatenate([keep, indices], 0)
    there = swap(jnp.concatenate([send, indices], 0), "yl")
    pair = jnp.concatenate([here, there], 1)
    first, second, pair_indices = pair[:32], pair[32:64], pair[64:]
    keep = jnp.where(core_at == 0, first, second)
    send = jnp.where(core_at == 0, second, first)
    beside = swap(jnp.concatenate([send, pair_indices], 0), "core")
    radial_rows = jnp.concatenate([keep, beside[:32]], 1)
    miller_rows = jnp.concatenate([pair_indices, beside[32:]], 1)
    classes = class_sums(miller_rows, radial_rows, scale, min(1024, 4 * waves))

    part = factors(pick, positions, features, cotangent, min(block, atoms // 2), 1)
    part = sum_scatter(part, ("x", "yh"))
    part = sum_everywhere(part, "z")
    total = gather(part, ("x", "yh"))
    grad, uv = feature_rows(positions, total, classes, atoms)
    grad_y, grad_core = swap(grad, "yl"), swap(grad, "core")
    total = lax.optimization_barrier((total, grad))[0]
    own, across, beside, far = filter_rows(miller_rows, total, scale)
    uv = lax.optimization_barrier((uv, own))[0]
    across, beside, far = swap(across, "yl"), swap(beside, "core"), swap_both(far)
    posg = position_rows(pick, positions, features, cotangent, uv, min(block, atoms))
    across, far, grad_y, posg = lax.optimization_barrier((across, far, grad_y, posg))
    grad_far = swap(grad_y, "core")
    posg_far, posg_y, posg_core = swap_both(posg), swap(posg, "yl"), swap(posg, "core")
    feature_grad, filter_grad = place_rows(pick, (grad, grad_core, grad_y, grad_far), (own, beside, across, far))
    posg_far, posg_y, posg_core, filter_grad = lax.optimization_barrier((posg_far, posg_y, posg_core, filter_grad))
    position_grad = (posg + posg_core) + (posg_y + posg_far)
    return feature_grad, position_grad, filter_grad


def solution(mesh):
    x, yh = 4, 2
    z = mesh.shape["atom"] // (x * yh)
    fine = Mesh(mesh.devices.reshape(z, yh, x, 2, 2), ("z", "yh", "x", "yl", "core"))
    atom, wave = ("z", "yh", "x"), ("yl", "core")
    placed = (P(None, atom), P(atom, None), P(atom, None), P(None, wave), P(wave, None))
    return jax.shard_map(
        functools.partial(shards, 2048),
        mesh=fine,
        in_specs=placed,
        out_specs=(P(atom, None), P(None, atom), P(wave, None)),
        check_vma=False,
    )
```

```python
import functools
import math

import jax
import jax.numpy as jnp
from jax import lax
from jax.experimental import pallas as pl
from jax.experimental.pallas import tpu as pltpu
from jax.sharding import Mesh, PartitionSpec as P

phase_step = 2.0 * math.pi / 256.0
PAIRS = 296
PAIR_ROWS = 304
TILES = 9
SLOTS = 17 * 64
CLASSES = 896
PACKED = 2560
f32 = jnp.float32
bf16 = jnp.bfloat16
MIB = 1024 * 1024


def nt_dot(a, b):
    return lax.dot_general(a, b, (((1,), (1,)), ((), ())), preferred_element_type=f32)


def turn_trig(turns):
    x = (turns - jnp.floor(turns + 0.5)) * (2.0 * math.pi)
    square = x * x
    cosine = jnp.full_like(x, 1.0 / math.factorial(18) * -1.0)
    for power in range(16, -1, -2):
        cosine = cosine * square + ((-1.0) ** (power // 2) / math.factorial(power))
    sine = jnp.full_like(x, 1.0 / math.factorial(17))
    for power in range(15, 0, -2):
        sine = sine * square + ((-1.0) ** (power // 2) / math.factorial(power))
    return cosine, sine * x


def multiples(position_rows):
    count = position_rows.shape[1]
    orders = lax.broadcasted_iota(jnp.int32, (8, count), 0).astype(f32) + 1.0
    return [turn_trig(orders * (position_rows[d : d + 1, :] * (1.0 / 256.0))) for d in range(3)]


def pair_table(trig1, trig2):
    (c1, s1), (c2, s2) = trig1, trig2
    count = c1.shape[1]
    tiles = []
    for left in (c1, s1):
        for right in (c2, s2):
            for m in range(8):
                tiles.append(left[m : m + 1, :] * right)
    one = (lax.broadcasted_iota(jnp.int32, (16, count), 0) == 0).astype(f32)
    tiles += [c2, s2, c1, s1, one]
    return jnp.concatenate(tiles, 0)


def row_tables(pick_ref, features, cotangent):
    lane = lax.broadcasted_iota(jnp.int32, (32, 128), 1)
    row = lax.broadcasted_iota(jnp.int32, (32, 128), 0)
    pick = (lane == row + 32 * pick_ref[0]).astype(bf16)
    return jnp.concatenate([nt_dot(pick, features), nt_dot(pick, cotangent)], 0)


def fill_slots(slots_ref, trig0, rows):
    c0, s0 = trig0
    for t in range(8):
        slots_ref[128 * t : 128 * t + 64, :] = (c0[t : t + 1, :] * rows).astype(bf16)
        slots_ref[128 * t + 64 : 128 * t + 128, :] = (s0[t : t + 1, :] * rows).astype(bf16)
    slots_ref[1024:1088, :] = rows.astype(bf16)


def factor_kernel(pick_ref, pos_ref, feat_ref, cot_ref, out_ref, total_ref, *slots_refs):
    step = pl.program_id(0)
    size = slots_refs[0].shape[1]
    product = None
    for k, slots_ref in enumerate(slots_refs):
        at = slice(k * size, (k + 1) * size)
        trig = multiples(pos_ref[:, at])
        fill_slots(slots_ref, trig[0], row_tables(pick_ref, feat_ref[at, :], cot_ref[at, :]))
        pairs = pair_table(trig[1], trig[2]).astype(bf16)
        part = nt_dot(pairs, slots_ref[...])
        product = part if product is None else product + part

    @pl.when(step == 0)
    def _():
        total_ref[...] = product

    final = pl.num_programs(0) - 1

    @pl.when(jnp.logical_and(step > 0, step < final))
    def _():
        total_ref[...] += product

    @pl.when(step == final)
    def _():
        for t in range(8):
            at = slice(128 * t, 128 * t + 128)
            out_ref[PAIRS * t : PAIRS * (t + 1), :] = total_ref[0:PAIRS, at] + product[0:PAIRS, at]
        last = total_ref[:, 1024:1088] + product[:, 1024:1088]
        out_ref[2368:2520, :] = jnp.concatenate([last[0:152], last[152:304]], 1)
        out_ref[2520:2560, :] = jnp.zeros((40, 128), f32)


def factors(pick, positions, features, cotangent, block, cuts):
    atoms = positions.shape[1]
    return pl.pallas_call(
        factor_kernel,
        grid=(atoms // block,),
        in_specs=[
            pl.BlockSpec(memory_space=pltpu.SMEM),
            pl.BlockSpec((3, block), lambda i: (0, i)),
            pl.BlockSpec((block, 128), lambda i: (i, 0)),
            pl.BlockSpec((block, 128), lambda i: (i, 0)),
        ],
        out_specs=pl.BlockSpec((PACKED, 128), lambda i: (0, 0)),
        out_shape=jax.ShapeDtypeStruct((PACKED, 128), f32),
        scratch_shapes=[pltpu.VMEM((PAIR_ROWS, SLOTS), f32)] + [pltpu.VMEM((SLOTS, block // cuts), bf16)] * cuts,
        compiler_params=pltpu.CompilerParams(vmem_limit_bytes=56 * MIB),
        cost_estimate=pl.CostEstimate(flops=2 * PAIR_ROWS * SLOTS * atoms, bytes_accessed=atoms * 520, transcendentals=0),
        name="factors",
    )(pick, positions, features, cotangent)


def wave_class(m):
    m0, m1, m2 = [m[d : d + 1, :] for d in range(3)]
    size0, size1, size2 = jnp.abs(m0), jnp.abs(m1), jnp.abs(m2)
    signs = [jnp.clip(v, -1.0, 1.0) for v in (m0, m1, m2)]
    both = (size1 - 1.0) * 8.0 + size2 - 1.0
    inner = jnp.where(
        size1 > 0.0,
        jnp.where(size2 > 0.0, both, 72.0 + size1 - 1.0),
        jnp.where(size2 > 0.0, 64.0 + size2 - 1.0, 80.0),
    )
    tile = jnp.where(size0 > 0.0, size0 - 1.0, 8.0)
    index = (tile * 88.0 + inner).astype(jnp.int32)
    return index, (signs[1] * signs[2], signs[0] * signs[1], signs[0] * signs[2])


def split_hi_lo(v):
    hi = v.astype(bf16)
    return hi, (v - hi.astype(f32)).astype(bf16)


def class_kernel(scale, miller_ref, radial_ref, out_ref, sum_ref):
    step = pl.program_id(0)
    index, products = wave_class(miller_ref[0:3, :])
    radial = radial_ref[...]
    signed = jnp.concatenate([radial] + [radial * p for p in products], 0)
    hi, lo = split_hi_lo(signed)
    hot = (lax.broadcasted_iota(jnp.int32, (CLASSES, index.shape[1]), 0) == index).astype(f32).astype(bf16)
    part = nt_dot(hot, jnp.concatenate([hi, lo], 0))
    part = part[:, :128] + part[:, 128:]

    @pl.when(step == 0)
    def _():
        sum_ref[...] = part

    @pl.when(step > 0)
    def _():
        sum_ref[...] += part

    @pl.when(step == pl.num_programs(0) - 1)
    def _():
        for q in range(4):
            one = sum_ref[:, 32 * q : 32 * q + 32] * scale
            out_ref[q] = jnp.concatenate([one, one, one, one], 1)


def class_sums(miller_rows, radial_rows, scale, block):
    waves = miller_rows.shape[1]
    return pl.pallas_call(
        functools.partial(class_kernel, scale),
        grid=(waves // block,),
        in_specs=[pl.BlockSpec((8, block), lambda i: (0, i)), pl.BlockSpec((32, block), lambda i: (0, i))],
        out_specs=pl.BlockSpec((4, CLASSES, 128), lambda i: (0, 0, 0)),
        out_shape=jax.ShapeDtypeStruct((4, CLASSES, 128), f32),
        scratch_shapes=[pltpu.VMEM((CLASSES, 128), f32)],
        compiler_params=pltpu.CompilerParams(vmem_limit_bytes=18 * MIB),
        cost_estimate=pl.CostEstimate(flops=2 * CLASSES * 256 * waves, bytes_accessed=waves * 160, transcendentals=0),
        name="class_sums",
    )(miller_rows, radial_rows)


def load_tile(total_ref, t):
    if t < 8:
        return total_ref[PAIRS * t : PAIRS * (t + 1), :]
    fold = total_ref[2368:2520, :]
    last = jnp.concatenate([fold[:, :64], fold[0:144, 64:]], 0)
    return jnp.concatenate([last, jnp.zeros((PAIRS, 64), f32)], 1)


def lane_signs():
    lane = lax.broadcasted_iota(jnp.int32, (1, 128), 1)
    return lane, jnp.where(lane < 64, 1.0, -1.0).astype(f32)


def cut(v):
    return [v[0:64], v[64:128], v[128:192], v[192:256]] + [v[256 + 8 * k : 264 + 8 * k] for k in range(5)]


def combine(total_ref, class_ref, uv_ref, down_ref):
    lane, half = lane_signs()
    swap = (lane % 64) < 32
    pick_lane = lax.broadcasted_iota(jnp.int32, (64, 128), 1)
    pick_row = lax.broadcasted_iota(jnp.int32, (64, 128), 0)
    pick = (pick_lane == jnp.where(pick_row < 32, pick_row + 32, pick_row + 64)).astype(bf16)
    for t in range(TILES):
        a = load_tile(total_ref, t)
        x0, x1, x2, x3 = [class_ref[q, 88 * t : 88 * t + 88, :] for q in range(4)]
        i0, i1, i2, i3 = [v[0:64] for v in (x0, x1, x2, x3)]
        cc, cs, sc, ss, e2c, e2s, e1c, e1s, co = cut(a)
        f0, f3 = x0[64:72], x3[64:72]
        g0, g2 = x0[72:80], x2[72:80]
        if t < 8:
            bcc, bcs, bsc, bss, be2c, be2s, be1c, be1s, _ = cut(half * pltpu.roll(a, 64, 1))
            blocks = [
                i0 * cc - i1 * ss - i2 * bsc - i3 * bcs,
                i0 * cs + i1 * sc - i2 * bss + i3 * bcc,
                i0 * sc + i1 * cs + i2 * bcc - i3 * bss,
                i0 * ss - i1 * cc + i2 * bcs + i3 * bsc,
                f0 * e2c - f3 * be2s,
                f0 * e2s + f3 * be2c,
                g0 * e1c - g2 * be1s,
                g0 * e1s + g2 * be1c,
            ]
        else:
            blocks = [i0 * cc - i1 * ss, i0 * cs + i1 * sc, i0 * sc + i1 * cs, i0 * ss - i1 * cc]
            blocks += [f0 * e2c, f0 * e2s, g0 * e1c, g0 * e1s]
        w = jnp.concatenate(blocks + [x0[80:88] * co, jnp.zeros((8, 128), f32)], 0)
        swapped = jnp.where(swap, pltpu.roll(w, 96, 1), pltpu.roll(w, 32, 1))
        uv_ref[0:PAIR_ROWS, 128 * t : 128 * t + 128] = swapped.astype(bf16)
        if t < 8:
            slope = (t + 1.0) * half * pltpu.roll(swapped, 64, 1)
        else:
            slope = jnp.zeros((PAIR_ROWS, 128), f32)
        uv_ref[PAIR_ROWS : 2 * PAIR_ROWS, 128 * t : 128 * t + 128] = slope.astype(bf16)
        down_ref[64 * t : 64 * t + 64, :] = nt_dot(pick, w.astype(bf16)).astype(bf16)


def pair_products(total_ref, pair_ref):
    _, half = lane_signs()
    pair_ref[:, 88 * TILES :, :] = jnp.zeros((4, CLASSES - 88 * TILES, 128), f32)
    for t in range(TILES):
        a = load_tile(total_ref, t)
        b = half * pltpu.roll(a, 64, 1)
        sa = pltpu.roll(a, 32, 1)
        sb = pltpu.roll(b, 32, 1)
        cc, cs, sc, ss, e2c, e2s, e1c, e1s, co = cut(a)
        scc, scs, ssc, sss, se2c, se2s, se1c, se1s, sco = cut(sa)
        tcc, tcs, tsc, tss, te2c, te2s, te1c, te1s, _ = cut(sb)
        zero = jnp.zeros((8, 128), f32)
        y = [
            [cc * scc + cs * scs + sc * ssc + ss * sss, e2c * se2c + e2s * se2s, e1c * se1c + e1s * se1s, co * sco],
            [cs * ssc + sc * scs - cc * sss - ss * scc, zero, zero, zero],
            [sc * tcc + ss * tcs - cc * tsc - cs * tss, zero, e1s * te1c - e1c * te1s, zero],
            [cs * tcc + ss * tsc - cc * tcs - sc * tss, e2s * te2c - e2c * te2s, zero, zero],
        ]
        for q in range(4):
            pair_ref[q, 88 * t : 88 * t + 88, :] = jnp.concatenate(y[q], 0)


def filter_kernel(scale, miller_ref, total_ref, *refs):
    *out_refs, pair_ref, turned_ref = refs
    step = pl.program_id(0)

    @pl.when(step == 0)
    def _():
        pair_products(total_ref, pair_ref)
        lane = lax.broadcasted_iota(jnp.int32, (32, 128), 1)
        row = lax.broadcasted_iota(jnp.int32, (32, 128), 0)
        pick = jnp.logical_or(lane == row + 32, lane == row + 96).astype(bf16)
        for q in range(4):
            turned_ref[32 * q : 32 * q + 32, :] = nt_dot(pick, pair_ref[q].astype(bf16)).astype(bf16)

    index, products = wave_class(miller_ref[0:3, :])
    hot = (lax.broadcasted_iota(jnp.int32, (CLASSES, index.shape[1]), 0) == index).astype(f32).astype(bf16)
    values = jnp.dot(turned_ref[...], hot, preferred_element_type=f32)
    rows = values[0:32]
    for q in range(3):
        rows = rows + products[q] * values[32 * (q + 1) : 32 * (q + 2)]
    rows = scale * rows

    for k, out_ref in enumerate(out_refs):

        @pl.when(step == k)
        def _():
            out_ref[...] = rows


def filter_rows(miller_rows, total, scale):
    block = miller_rows.shape[1] // 4
    one = jax.ShapeDtypeStruct((32, block), f32)
    return pl.pallas_call(
        functools.partial(filter_kernel, scale),
        grid=(4,),
        in_specs=[pl.BlockSpec((8, block), lambda i: (0, i)), pl.BlockSpec((PACKED, 128), lambda i: (0, 0))],
        out_specs=(pl.BlockSpec((32, block), lambda i: (0, 0)),) * 4,
        out_shape=(one,) * 4,
        scratch_shapes=[pltpu.VMEM((4, CLASSES, 128), f32), pltpu.VMEM((128, CLASSES), bf16)],
        compiler_params=pltpu.CompilerParams(vmem_limit_bytes=18 * MIB),
        cost_estimate=pl.CostEstimate(flops=2 * CLASSES * 1024 * block, bytes_accessed=block * 640, transcendentals=0),
        name="filter_rows",
    )(miller_rows, total)


def feature_kernel(pos_ref, total_ref, class_ref, grad_ref, uv_ref, down_ref):
    @pl.when(pl.program_id(0) == 0)
    def _():
        combine(total_ref, class_ref, uv_ref, down_ref)

    (c0, s0), trig1, trig2 = multiples(pos_ref[...])
    pairs = pair_table(trig1, trig2).astype(bf16)
    parts = jnp.dot(down_ref[...], pairs, preferred_element_type=f32)
    grad = parts[512:544]
    for t in range(8):
        grad = grad + c0[t : t + 1, :] * parts[64 * t : 64 * t + 32] + s0[t : t + 1, :] * parts[64 * t + 32 : 64 * t + 64]
    grad_ref[...] = grad


def feature_rows(positions, total, classes, block):
    atoms = positions.shape[1]
    return pl.pallas_call(
        feature_kernel,
        grid=(atoms // block,),
        in_specs=[
            pl.BlockSpec((3, block), lambda i: (0, i)),
            pl.BlockSpec((PACKED, 128), lambda i: (0, 0)),
            pl.BlockSpec((4, CLASSES, 128), lambda i: (0, 0, 0)),
        ],
        out_specs=(
            pl.BlockSpec((32, block), lambda i: (0, i)),
            pl.BlockSpec((2 * PAIR_ROWS, 128 * TILES), lambda i: (0, 0)),
        ),
        out_shape=(
            jax.ShapeDtypeStruct((32, atoms), f32),
            jax.ShapeDtypeStruct((2 * PAIR_ROWS, 128 * TILES), bf16),
        ),
        scratch_shapes=[pltpu.VMEM((64 * TILES, PAIR_ROWS), bf16)],
        compiler_params=pltpu.CompilerParams(vmem_limit_bytes=38 * MIB),
        cost_estimate=pl.CostEstimate(flops=2 * PAIR_ROWS * SLOTS * atoms, bytes_accessed=atoms * 700, transcendentals=0),
        name="feature_rows",
    )(positions, total, classes)


def position_kernel(pick_ref, pos_ref, feat_ref, cot_ref, uv_ref, posg_ref, slots_ref):
    trig = multiples(pos_ref[...])
    fill_slots(slots_ref, trig[0], row_tables(pick_ref, feat_ref[...], cot_ref[...]))
    both = jnp.dot(uv_ref[:, 0:1024], slots_ref[0:1024, :], preferred_element_type=f32)
    last = jnp.dot(uv_ref[0:PAIR_ROWS, 1024:SLOTS], slots_ref[1024:SLOTS, :], preferred_element_type=f32)
    posg_ref[...] = position_sums(trig, both[0:PAIR_ROWS] + last, both[PAIR_ROWS:])


def place_kernel(pick_ref, *refs):
    place = pick_ref[0]
    out_refs, all_refs = refs[8:10], refs[10:12]
    for k, (out_ref, all_ref) in enumerate(zip(out_refs, all_refs)):
        for flip, part_ref in enumerate(refs[4 * k : 4 * k + 4]):
            all_ref[pl.ds(pl.multiple_of(32 * jnp.bitwise_xor(place, flip), 32), 32), :] = part_ref[...]
        rows = out_ref.shape[0]
        width = min(512, rows)
        for at in range(0, rows, width):
            out_ref[at : at + width, :] = all_ref[:, at : at + width].T


def place_rows(pick, first, second):
    shapes = [first[0].shape, second[0].shape]
    whole = lambda shape: pl.BlockSpec(shape, lambda: (0, 0))
    return pl.pallas_call(
        place_kernel,
        in_specs=[pl.BlockSpec(memory_space=pltpu.SMEM)] + [whole(s) for s in shapes for _ in range(4)],
        out_specs=tuple(whole((s[1], 128)) for s in shapes),
        out_shape=tuple(jax.ShapeDtypeStruct((s[1], 128), f32) for s in shapes),
        scratch_shapes=[pltpu.VMEM((128, s[1]), f32) for s in shapes],
        compiler_params=pltpu.CompilerParams(vmem_limit_bytes=20 * MIB),
        cost_estimate=pl.CostEstimate(flops=6 * 10**9, bytes_accessed=4 * 10**6, transcendentals=0),
        name="place_rows",
    )(pick, *first, *second)


def position_sums(trig, u, v):
    _, (c1, s1), (c2, s2) = trig
    orders = lax.broadcasted_iota(jnp.int32, c1.shape, 0).astype(f32) + 1.0
    acc0 = c2 * v[256:264] + s2 * v[264:272] + c1 * v[272:280] + s1 * v[280:288]
    acc1 = orders * (c1 * u[280:288] - s1 * u[272:280])
    acc2 = c2 * u[264:272] - s2 * u[256:264]
    for m in range(8):
        lead_c, lead_s = c1[m : m + 1, :], s1[m : m + 1, :]
        ucc, ucs, usc, uss = [u[64 * k + 8 * m : 64 * k + 8 * m + 8] for k in range(4)]
        vcc, vcs, vsc, vss = [v[64 * k + 8 * m : 64 * k + 8 * m + 8] for k in range(4)]
        acc0 = acc0 + lead_c * (c2 * vcc + s2 * vcs) + lead_s * (c2 * vsc + s2 * vss)
        acc1 = acc1 + float(m + 1) * (lead_c * (c2 * usc + s2 * uss) - lead_s * (c2 * ucc + s2 * ucs))
        acc2 = acc2 + lead_c * (c2 * ucs - s2 * ucc) + lead_s * (c2 * uss - s2 * usc)
    acc2 = acc2 * orders
    rows = [jnp.sum(acc0, 0, keepdims=True) + v[288:289], jnp.sum(acc1, 0, keepdims=True), jnp.sum(acc2, 0, keepdims=True)]
    return phase_step * jnp.concatenate(rows, 0)


def position_rows(pick, positions, features, cotangent, uv, block):
    atoms = positions.shape[1]
    return pl.pallas_call(
        position_kernel,
        grid=(atoms // block,),
        in_specs=[
            pl.BlockSpec(memory_space=pltpu.SMEM),
            pl.BlockSpec((3, block), lambda i: (0, i)),
            pl.BlockSpec((block, 128), lambda i: (i, 0)),
            pl.BlockSpec((block, 128), lambda i: (i, 0)),
            pl.BlockSpec((2 * PAIR_ROWS, 128 * TILES), lambda i: (0, 0)),
        ],
        out_specs=pl.BlockSpec((3, block), lambda i: (0, i)),
        out_shape=jax.ShapeDtypeStruct((3, atoms), f32),
        scratch_shapes=[pltpu.VMEM((SLOTS, block), bf16)],
        compiler_params=pltpu.CompilerParams(vmem_limit_bytes=24 * MIB),
        cost_estimate=pl.CostEstimate(flops=4 * PAIR_ROWS * SLOTS * atoms, bytes_accessed=atoms * 700, transcendentals=0),
        name="position_rows",
    )(pick, positions, features, cotangent, uv)


def swap(value, axis):
    return lax.ppermute(value, axis, [(0, 1), (1, 0)])


def swap_both(value):
    return lax.ppermute(value, ("yl", "core"), [(i, 3 - i) for i in range(4)])


def sum_scatter(value, axis):
    n = lax.axis_size(axis)
    parts = lax.all_to_all(value.reshape(n, value.shape[0] // n, 128), axis, 0, 0)
    return jnp.sum(parts, 0)


def total_kernel(parts_ref, out_ref):
    total = jnp.sum(parts_ref[...], 0)
    for k in range(out_ref.shape[0]):
        out_ref[k] = total


def sum_everywhere(value, axis):
    n = lax.axis_size(axis)
    parts = lax.all_to_all(value.reshape(n, value.shape[0] // n, 128), axis, 0, 0)
    copies = pl.pallas_call(
        total_kernel,
        out_shape=jax.ShapeDtypeStruct(parts.shape, f32),
        compiler_params=pltpu.CompilerParams(vmem_limit_bytes=4 * MIB),
        name="total_rows",
    )(parts)
    return lax.all_to_all(copies, axis, 0, 0).reshape(value.shape)


def gather(value, axis):
    n = lax.axis_size(axis)
    copies = jnp.broadcast_to(value[None], (n,) + value.shape)
    return lax.all_to_all(copies, axis, 0, 0).reshape(n * value.shape[0], 128)


def shards(block, positions, features, cotangent, miller, radial_filter):
    atoms = positions.shape[1]
    block = min(block, atoms)
    waves = miller.shape[1]
    y_at, core_at = lax.axis_index("yl"), lax.axis_index("core")
    atom_count = atoms * lax.axis_size(("z", "yh", "x"))
    wave_count = waves * lax.axis_size(("yl", "core"))
    scale = float(atom_count * wave_count) ** (-0.5)
    pick = (2 * y_at + core_at).astype(jnp.int32).reshape(1)

    turned = radial_filter.T.reshape(2, 64, waves)
    indices = jnp.concatenate([miller.astype(f32), jnp.zeros((5, waves), f32)], 0)
    keep = jnp.where(y_at == 0, turned[0], turned[1])
    send = jnp.where(y_at == 0, turned[1], turned[0])
    here = jnp.concatenate([keep, indices], 0)
    there = swap(jnp.concatenate([send, indices], 0), "yl")
    pair = jnp.concatenate([here, there], 1)
    first, second, pair_indices = pair[:32], pair[32:64], pair[64:]
    keep = jnp.where(core_at == 0, first, second)
    send = jnp.where(core_at == 0, second, first)
    beside = swap(jnp.concatenate([send, pair_indices], 0), "core")
    radial_rows = jnp.concatenate([keep, beside[:32]], 1)
    miller_rows = jnp.concatenate([pair_indices, beside[32:]], 1)
    classes = class_sums(miller_rows, radial_rows, scale, min(1024, 4 * waves))

    part = factors(pick, positions, features, cotangent, min(block, atoms // 2), 1)
    part = sum_scatter(part, ("x", "yh"))
    part = sum_everywhere(part, "z")
    total = gather(part, ("x", "yh"))
    grad, uv = feature_rows(positions, total, classes, atoms // 2)
    grad_y, grad_core = swap(grad, "yl"), swap(grad, "core")
    total = lax.optimization_barrier((total, grad))[0]
    own, across, beside, far = filter_rows(miller_rows, total, scale)
    uv = lax.optimization_barrier((uv, own))[0]
    across, beside, far = swap(across, "yl"), swap(beside, "core"), swap_both(far)
    posg = position_rows(pick, positions, features, cotangent, uv, min(block, atoms))
    across, far, grad_y, posg = lax.optimization_barrier((across, far, grad_y, posg))
    grad_far = swap(grad_y, "core")
    posg_far, posg_y, posg_core = swap_both(posg), swap(posg, "yl"), swap(posg, "core")
    feature_grad, filter_grad = place_rows(pick, (grad, grad_core, grad_y, grad_far), (own, beside, across, far))
    posg_far, posg_y, posg_core, filter_grad = lax.optimization_barrier((posg_far, posg_y, posg_core, filter_grad))
    position_grad = (posg + posg_core) + (posg_y + posg_far)
    return feature_grad, position_grad, filter_grad


def solution(mesh):
    x, yh = 4, 2
    z = mesh.shape["atom"] // (x * yh)
    fine = Mesh(mesh.devices.reshape(z, yh, x, 2, 2), ("z", "yh", "x", "yl", "core"))
    atom, wave = ("z", "yh", "x"), ("yl", "core")
    placed = (P(None, atom), P(atom, None), P(atom, None), P(None, wave), P(wave, None))
    return jax.shard_map(
        functools.partial(shards, 2048),
        mesh=fine,
        in_specs=placed,
        out_specs=(P(atom, None), P(None, atom), P(wave, None)),
        check_vma=False,
    )
```
